512 devices in a mesh: sec: 8 (over z_hi, core), tile: 64 (over z_lo, x, y).
Axes of the slice: x: 4, y: 4, z: 16 (z_hi: 4, z_lo: 4; z = z_hi * 4 + z_lo), core: 2. Of those that a mesh axis runs over, the one named last changes fastest.
Arguments:
- displacement: float32 [8, 2, 128, 4096], P('sec', None, 'tile'), may hold values from -6 to 6
- stiffness: float32 [8, 128, 4096], P('sec', 'tile'), may hold values from 0.5 to 2
- match_weight: float32 [8, 192, 512], P('sec', 'tile'), may hold values from 0.5 to 4
- match_offset: float32 [8, 2, 192, 512], P('sec', None, 'tile'), may hold values from -6 to 6
- source_row: int32 [8, 192, 512], P('sec', 'tile'), may hold values from 0 to 1
- source_col: int32 [8, 192, 512], P('sec', 'tile'), may hold values from 0 to 4095
- target_row: int32 [8, 192, 512], P('sec', 'tile'), may hold values from 0 to 1
- target_col: int32 [8, 192, 512], P('sec', 'tile'), may hold values from 0 to 4095
- match_count: int32 [8, 192], P('sec', 'tile'), may hold values from 0 to 512, as said below
Outputs:
- aligned: float32 [8, 2, 128, 4096], P('sec', None, 'tile')
The draws below stay inside these ranges and needn't reach their ends.
Inputs may be any that keep to these rules, and one draw needn't show every extreme that they name: `match_count`: in every section some tile's group 1 uses all 512 slots, and some tile other than the first and the last uses all 512 slots in group 0 and in group 2.
All inputs are finite; a program needn't handle non-finite values.
Results may differ from the reference program's by a relative error of at most 0.0018.
Values sent between devices are 32-bit elements; how exact they have to be, the bound alone decides.
No kernel may reach another device: no remote copies, remote signals or barrier semaphores. Data moves between devices by JAX's collectives and lax.ppermute only.
A program may use at most 64 MiB of HBM per device.

```python
import math
import jax
import jax.numpy as jnp
from jax import lax

W = 4096
ROWS_DEV = 2
MATCH = 512
STEPS = 2
SECTIONS = 8
NROWS = 128
N_TILE = 64


def draw_match_count(key, part):
    key_own, key_edge, key_pick, key_side = jax.random.split(jax.random.fold_in(key, 17), 4)
    own = jax.random.randint(key_own, (SECTIONS, N_TILE), MATCH // 4, MATCH + 1)
    edge = jax.random.randint(key_edge, (SECTIONS, N_TILE, 2), MATCH // 8, MATCH + 1)
    picked = jax.random.randint(key_pick, (SECTIONS,), 0, N_TILE)
    side_pick = jax.random.randint(key_side, (SECTIONS,), 1, N_TILE - 1)
    tiles = jnp.arange(N_TILE)
    own = jnp.where(tiles[None, :] == picked[:, None], MATCH, own)
    edge = jnp.where((tiles[None, :] == side_pick[:, None])[..., None], MATCH, edge)
    counts = jnp.stack([edge[..., 0], own, edge[..., 1]], axis=-1)
    return counts.reshape(SECTIONS, 3 * N_TILE).astype(jnp.int32)


def with_ends(entries, own_key, least, largest):
    place = [jax.random.randint(jax.random.fold_in(own_key, axis), (), 0, length) for axis, length in enumerate(entries.shape)]
    widest = entries.shape.index(max(entries.shape))
    next_to = place[:widest] + [(place[widest] + 1) % entries.shape[widest]] + place[widest + 1:]
    return entries.at[tuple(place)].set(least).at[tuple(next_to)].set(largest)


def block_scale(rng, shape, cuts, least, top_value):
    factor_of = 1.0
    for axis_at, shards_of in cuts:
        draws = jax.random.uniform(jax.random.fold_in(jax.random.fold_in(rng, 6), axis_at), (shards_of,), jnp.float32, least / len(cuts), top_value / len(cuts))
        factor_of = factor_of * jnp.repeat(jnp.exp(draws), shape[axis_at] // shards_of).reshape((-1,) + (1,) * (len(shape) - 1 - axis_at))
    return factor_of


def normal_values(key, shape, deviation, bound, cuts=(), kind=jnp.bfloat16):
    result = jax.random.normal(key, shape, jnp.float32) * deviation
    if len(cuts) > 0:
        result = block_scale(key, shape, cuts, -0.22, 0.18) * result
    return jnp.clip(result, min=-bound, max=bound).astype(kind)


def setup_inputs(seed: int = 0) -> dict:
    key_of = jax.random.split(jax.random.key(seed), 10)
    return {
        "displacement": normal_values(key_of[0], (SECTIONS, 2, NROWS, W), 1.0, 6.0, ((0, 8), (2, 64)), jnp.float32),
        "stiffness": jnp.clip(jnp.exp(math.log(2.0) - 1.3862944 * jax.random.uniform(key_of[1], (SECTIONS, NROWS, W), jnp.float32) ** block_scale(key_of[1], (SECTIONS, NROWS, W), ((0, 8), (1, 64)), -0.2, 0.2)), 0.5, 2.0),
        "match_weight": jnp.clip(jnp.exp(math.log(4.0) - 2.0794415 * jax.random.uniform(key_of[2], (SECTIONS, 3 * N_TILE, MATCH), jnp.float32) ** block_scale(key_of[2], (SECTIONS, 3 * N_TILE, MATCH), ((0, 8), (1, 64)), -0.2, 0.2)), 0.5, 4.0),
        "match_offset": normal_values(key_of[3], (SECTIONS, 2, 3 * N_TILE, MATCH), 1.0, 6.0, ((0, 8), (2, 64)), jnp.float32),
        "source_row": with_ends(jax.random.randint(key_of[4], (SECTIONS, 3 * N_TILE, MATCH), 0, ROWS_DEV), jax.random.fold_in(key_of[4], 1), 0, ROWS_DEV - 1).astype(jnp.int32),
        "source_col": with_ends(jax.random.randint(key_of[5], (SECTIONS, 3 * N_TILE, MATCH), 0, W), jax.random.fold_in(key_of[5], 1), 0, W - 1).astype(jnp.int32),
        "target_row": with_ends(jax.random.randint(key_of[6], (SECTIONS, 3 * N_TILE, MATCH), 0, ROWS_DEV), jax.random.fold_in(key_of[6], 1), 0, ROWS_DEV - 1).astype(jnp.int32),
        "target_col": with_ends(jax.random.randint(key_of[7], (SECTIONS, 3 * N_TILE, MATCH), 0, W), jax.random.fold_in(key_of[7], 1), 0, W - 1).astype(jnp.int32),
        "match_count": draw_match_count(jax.random.fold_in(key_of[9], 71), 0),
    }


neighbours = [(-1, 0, 1.0), (1, 0, 1.0), (0, -1, 1.0), (0, 1, 1.0), (-1, -1, 0.5), (-1, 1, 0.5), (1, -1, 0.5), (1, 1, 0.5)]
damping = 0.7


def springs(padded_u, padded_c, field, stiff_now):
    row_count = field.shape[1]
    col_count = field.shape[2]
    force = jnp.zeros_like(field)
    total = jnp.zeros_like(stiff_now)
    for row_shift, col_shift, factor in neighbours:
        near_u = padded_u[:, 1 + row_shift:1 + row_shift + row_count, 1 + col_shift:1 + col_shift + col_count]
        near_c = padded_c[1 + row_shift:1 + row_shift + row_count, 1 + col_shift:1 + col_shift + col_count]
        spring = factor * stiff_now * near_c
        force = force + spring[None] * (near_u - field)
        total = total + spring
    return force, total


def section_springs(pair):
    field, stiff_now = pair
    padded_u = jnp.pad(field, ((0, 0), (1, 1), (1, 1)))
    padded_c = jnp.pad(stiff_now, ((1, 1), (1, 1)))
    return springs(padded_u, padded_c, field, stiff_now)


def reference(displacement, stiffness, match_weight, match_offset, source_row, source_col, target_row, target_col, match_count):
    n_sec = SECTIONS
    n_tile = N_TILE
    slots = MATCH
    sections = jnp.arange(n_sec).astype(jnp.int32)
    tiles = jnp.arange(n_tile).astype(jnp.int32)
    groups = jnp.arange(3).astype(jnp.int32)
    slot_ids = jnp.arange(slots).astype(jnp.int32)
    counts = match_count.reshape(n_sec, n_tile, 3)
    dest_tile = tiles[:, None] + groups[None, :] - 1
    tile_ok = (dest_tile >= 0) & (dest_tile < n_tile)
    usable = (slot_ids[None, None, None, :] < counts[..., None]) & (sections[:, None, None, None] < n_sec - 1) & tile_ok[None, :, :, None]
    weight = jnp.where(usable, match_weight.reshape(n_sec, n_tile, 3, slots), jnp.float32(0.0))
    offset = match_offset.reshape(n_sec, 2, n_tile, 3, slots).transpose(1, 0, 2, 3, 4).reshape(2, -1)
    source_rows = tiles[None, :, None, None] * ROWS_DEV + source_row.reshape(n_sec, n_tile, 3, slots)
    source_idx = ((sections[:, None, None, None] * NROWS + source_rows) * W + source_col.reshape(n_sec, n_tile, 3, slots)).astype(jnp.int32)
    next_sec = jnp.clip(sections + 1, 0, n_sec - 1).astype(jnp.int32)
    dest_clip = jnp.clip(dest_tile, 0, n_tile - 1).astype(jnp.int32)
    recv_slot = (2 - groups).astype(jnp.int32)
    rows_arr = target_row.reshape(n_sec, n_tile, 3, slots)
    cols_arr = target_col.reshape(n_sec, n_tile, 3, slots)
    target_rows = rows_arr[next_sec[:, None, None], dest_clip[None, :, :], recv_slot[None, None, :]]
    target_cols = cols_arr[next_sec[:, None, None], dest_clip[None, :, :], recv_slot[None, None, :]]
    target_idx = ((next_sec[:, None, None, None] * NROWS + dest_clip[None, :, :, None] * ROWS_DEV + target_rows) * W + target_cols).astype(jnp.int32)
    source_idx = source_idx.reshape(-1)
    target_idx = target_idx.reshape(-1)
    weight = weight.reshape(-1)
    flat_u = displacement.transpose(1, 0, 2, 3).reshape(2, -1)
    for sweep_no in range(STEPS):
        fields = flat_u.reshape(2, n_sec, NROWS, W).transpose(1, 0, 2, 3)
        force, total = lax.map(section_springs, (fields, stiffness))
        flat_force = force.transpose(1, 0, 2, 3).reshape(2, -1)
        flat_total = total.reshape(-1)
        pull = weight[None] * (flat_u[:, target_idx] - (flat_u[:, source_idx] - offset))
        flat_force = flat_force.at[:, source_idx].add(pull)
        flat_force = flat_force.at[:, target_idx].add(-pull)
        flat_total = flat_total.at[source_idx].add(weight)
        flat_total = flat_total.at[target_idx].add(weight)
        flat_u = flat_u + damping * flat_force / flat_total[None]
    return flat_u.reshape(2, n_sec, NROWS, W).transpose(1, 0, 2, 3)
```

```python
import jax
import jax.numpy as jnp
from jax import lax
from jax.experimental import pallas as pl
from jax.experimental.pallas import tpu as pltpu
from jax.sharding import PartitionSpec as P

damping = 0.7
LANES = 128
F32 = jnp.float32
BF16 = jnp.bfloat16
VMEM = pl.BlockSpec(memory_space=pltpu.VMEM)
SMEM = pl.BlockSpec(memory_space=pltpu.SMEM)


def halves(value):
    high = value.astype(BF16)
    return high, (value - high.astype(F32)).astype(BF16)


def one_hot(index, depth):
    place = lax.broadcasted_iota(jnp.int32, (depth, index.shape[1]), 0)
    return place == index


def gather(table, lane_hot, block_mask):
    blocks = block_mask.shape[0]
    picked = jnp.dot(table, jnp.concatenate([lane_hot, lane_hot], axis=0), preferred_element_type=F32)
    return [
        jnp.sum(jnp.where(block_mask, picked[i * blocks : (i + 1) * blocks], 0.0), axis=0, keepdims=True)
        for i in range(picked.shape[0] // blocks)
    ]


def table_of(fields):
    high, low = halves(jnp.concatenate(fields, axis=0))
    return jnp.concatenate([high, low], axis=1)


def scatter(values, lane_hot, block_hot):
    parts = [halves(v) for v in values]
    left = jnp.concatenate([block_hot * p[k] for k in range(2) for p in parts], axis=0)
    return lax.dot_general(left, lane_hot, (((1,), (1,)), ((), ())), preferred_element_type=F32)


def wide(block):
    return jnp.concatenate([block[8 * i : 8 * i + 8] for i in range(4)], axis=1)


def narrow(rows):
    return jnp.concatenate([rows[:, LANES * i : LANES * (i + 1)] for i in range(4)], axis=0)


def side_sum(block):
    count = block.shape[0]
    lane = lax.broadcasted_iota(jnp.int32, block.shape, 1)
    row = lax.broadcasted_iota(jnp.int32, block.shape, 0)
    before = pltpu.roll(block, 1, 1)
    carried = jnp.where(row == 0, 0.0, pltpu.roll(before, 1, 0))
    before = jnp.where(lane == 0, carried, before)
    after = pltpu.roll(block, LANES - 1, 1)
    carried = jnp.where(row == count - 1, 0.0, pltpu.roll(after, count - 1, 0))
    after = jnp.where(lane == LANES - 1, carried, after)
    return before + after


def stencil(above, first, second, below):
    sides = [side_sum(b) for b in (above, first, second, below)]
    upper = first + 0.5 * sides[1]
    lower = second + 0.5 * sides[2]
    return jnp.concatenate(
        [
            above + 0.5 * sides[0] + lower + sides[1],
            upper + below + 0.5 * sides[3] + sides[2],
        ],
        axis=0,
    )


def rows_of(ref, lead=()):
    return [ref[lead + (pl.ds(r, 32, 2), slice(None))] for r in range(2)]


def fill(ref, rows):
    pad = (-len(rows)) % 8
    ref[...] = jnp.concatenate(rows + [jnp.zeros_like(rows[0])] * pad, axis=0)


def send_tiles(odd_tile, left, right, even_ref, odd_ref):
    even_ref[...] = jnp.where(odd_tile, left, right)
    odd_ref[...] = jnp.where(odd_tile, right, left)


def tile_message(halo, slot_rows):
    pad = (-len(slot_rows)) % 8
    rows = [wide(h) for h in halo] + slot_rows + [jnp.zeros_like(slot_rows[0])] * pad
    return jnp.concatenate(rows, axis=0)


def first_kernel(place, count, u, c, w, off, srow, scol, trow, tcol, even_msg, odd_msg, own, ids, uo, co):
    sec, tile, n_sec, n_tile = place[0], place[1], place[2], place[3]
    field = [jnp.concatenate(rows_of(u, (i,)), axis=0) for i in range(2)]
    stiff = jnp.concatenate(rows_of(c), axis=0)
    for i in range(2):
        uo[i] = field[i]
    co[...] = stiff
    table = table_of(field)
    slot = lax.broadcasted_iota(jnp.int32, (1, w.shape[1]), 1)
    sources, targets, blocks, lanes = [], [], [], []
    for g in range(3):
        dest = tile + g - 1
        limit = jnp.where((sec < n_sec - 1) & (dest >= 0) & (dest < n_tile), count[0, g], 0)
        weight = jnp.where(slot < limit, w[g : g + 1], 0.0)
        col = scol[g : g + 1]
        block, lane = srow[g : g + 1] * 32 + (col >> 7), col & 127
        blocks.append(block)
        lanes.append(lane)
        got = gather(table, one_hot(lane, LANES).astype(BF16), one_hot(block, 64))
        sources.append([weight * (got[i] - off[i, g : g + 1]) for i in range(2)] + [weight])
    for k in range(3):
        col = tcol[k : k + 1]
        block, lane = trow[k : k + 1] * 32 + (col >> 7), col & 127
        blocks.append(block)
        lanes.append(lane)
        targets.append(gather(table, one_hot(lane, LANES).astype(BF16), one_hot(block, 64)))
    halo = [stiff * field[0], stiff * field[1], stiff]
    left = tile_message([h[:32] for h in halo], sources[0] + targets[0])
    right = tile_message([h[32:] for h in halo], sources[2] + targets[2])
    send_tiles((tile & 1) == 1, left, right, even_msg, odd_msg)
    fill(own, sources[1] + targets[1] + [s[2] for s in sources])
    fill(ids, blocks + lanes)


def both_sides(place, even_in, odd_in, rows):
    odd_tile = (place[1] & 1) == 1
    mate = 1 - (place[1] & 1)
    even = even_in[mate, rows, :]
    odd = odd_in[rows, :]
    return jnp.where(odd_tile, even, odd), jnp.where(odd_tile, odd, even)


def pack_kernel(first, place, even_in, odd_in, own, even_msg, odd_msg):
    base = 24 if first else 16
    n_src = 3 if first else 2
    left, right = both_sides(place, even_in, odd_in, slice(base, base + 8))
    own_rows = own[...]
    source = [m[i : i + 1] for m in (left, own_rows, right) for i in range(n_src)]
    target = [m[n_src + i : n_src + i + 1] for m in (left, own_rows, right) for i in range(2)]
    size = even_msg.shape[0]
    zero = jnp.zeros_like(source[0])
    source = jnp.concatenate(source + [zero] * (size - len(source)), axis=0)
    target = jnp.concatenate(target + [zero] * (size - len(target)), axis=0)
    send_tiles((place[0] & 1) == 1, target, source, even_msg, odd_msg)


def spring_kernel(first, place, even_in, odd_in, u, c, *refs):
    stiff = c[...]
    up, down = both_sides(place, even_in, odd_in, slice(0, 24 if first else 16))
    if first:
        near_ref, total_ref = refs
        fields = [stiff * u[0], stiff * u[1], stiff]
    else:
        (near_ref,) = refs
        fields = [stiff * u[0], stiff * u[1]]
    for i, f in enumerate(fields):
        near = stiff * stencil(narrow(up[8 * i : 8 * i + 8]), f[:32], f[32:], narrow(down[8 * i : 8 * i + 8]))
        if i < 2:
            near_ref[i] = near
        else:
            total_ref[...] = near


def arrivals(place, even_in, odd_in):
    odd_sec = (place[0] & 1) == 1
    mate = 1 - (place[0] & 1)
    even = even_in[mate]
    odd = odd_in[...]
    return jnp.where(odd_sec, even, odd), jnp.where(odd_sec, odd, even)


def hot_of(ids, g):
    return one_hot(ids[6 + g : 7 + g], LANES), one_hot(ids[g : g + 1], 64)


def middle_kernel(place, even_in, odd_in, own, ids, off, u, c, near, total, u_out, total_out, even_msg, odd_msg, own_out):
    source_in, target_in = arrivals(place, even_in, odd_in)
    ids = ids[...]
    acc = jnp.zeros((384, LANES), F32)
    hots = []
    weights = []
    for g in range(3):
        weight = own[5 + g : 6 + g, :]
        weights.append(weight)
        vals = [weight * (target_in[2 * g + i : 2 * g + i + 1] + off[i, g : g + 1]) for i in range(2)] + [weight]
        lane_hot, block_mask = hot_of(ids, g)
        lane_hot = lane_hot.astype(BF16)
        hots.append((lane_hot, block_mask))
        acc = acc + scatter(vals, lane_hot, block_mask.astype(BF16))
    for k in range(3):
        vals = [source_in[3 * k + i : 3 * k + i + 1] for i in range(3)]
        lane_hot, block_mask = hot_of(ids, 3 + k)
        lane_hot = lane_hot.astype(BF16)
        hots.append((lane_hot, block_mask))
        acc = acc + scatter(vals, lane_hot, block_mask.astype(BF16))
    acc = acc[:192] + acc[192:]
    share = damping / (total[...] + acc[128:192])
    total_out[...] = share
    stiff = c[...]
    field = [(1.0 - damping) * u[i] + (near[i] + acc[64 * i : 64 * i + 64]) * share for i in range(2)]
    for i in range(2):
        u_out[i] = field[i]
    table = table_of(field)
    got = [gather(table, *h) for h in hots]
    sources = [[weights[g] * (got[g][i] - off[i, g : g + 1]) for i in range(2)] for g in range(3)]
    targets = got[3:]
    halo = [stiff * field[0], stiff * field[1]]
    left = tile_message([h[:32] for h in halo], sources[0] + targets[0])
    right = tile_message([h[32:] for h in halo], sources[2] + targets[2])
    send_tiles((place[1] & 1) == 1, left, right, even_msg, odd_msg)
    fill(own_out, sources[1] + targets[1])


def last_kernel(place, even_in, odd_in, own, ids, off, u, near, share, out):
    source_in, target_in = arrivals(place, even_in, odd_in)
    ids = ids[...]
    acc = jnp.zeros((256, LANES), F32)
    for g in range(6):
        if g < 3:
            weight = own[5 + g : 6 + g, :]
            vals = [weight * (target_in[2 * g + i : 2 * g + i + 1] + off[i, g : g + 1]) for i in range(2)]
        else:
            vals = [source_in[2 * (g - 3) + i : 2 * (g - 3) + i + 1] for i in range(2)]
        lane_hot, block_mask = hot_of(ids, g)
        acc = acc + scatter(vals, lane_hot.astype(BF16), block_mask.astype(BF16))
    acc = acc[:128] + acc[128:]
    for i in range(2):
        new = (1.0 - damping) * u[i] + (near[i] + acc[64 * i : 64 * i + 64]) * share[...]
        for r in range(2):
            out[i, pl.ds(r, 32, 2), :] = new[32 * r : 32 * r + 32]


def call(kernel, shapes, *args, scalars=1):
    return pl.pallas_call(
        kernel,
        out_shape=[jax.ShapeDtypeStruct(s, d) for s, d in shapes],
        in_specs=[SMEM] * scalars + [VMEM] * (len(args) - scalars),
        out_specs=[VMEM] * len(shapes),
        compiler_params=pltpu.CompilerParams(vmem_limit_bytes=32 * 1024 * 1024),
    )(*args)


def body(n_sec, n_tile, displacement, stiffness, match_weight, match_offset, source_row, source_col, target_row, target_col, match_count):
    axes = ("sec", "tile")
    slots = match_weight.shape[2]
    place = jnp.stack([lax.axis_index("sec"), lax.axis_index("tile"), jnp.int32(n_sec), jnp.int32(n_tile)])

    def flat(s, t):
        return s * n_tile + t

    tile_even = [[flat(s, t), flat(s, t + 1)] for s in range(n_sec) for t in range(0, n_tile, 2)]
    tile_odd = [[flat(s, t), flat(s, t + 1)] for s in range(n_sec) for t in range(1, n_tile - 1, 2)]
    sec_even = [[flat(s, t), flat(s + 1, t)] for s in range(0, n_sec, 2) for t in range(n_tile)]
    sec_odd = [[flat(s, t), flat(s + 1, t)] for s in range(1, n_sec - 1, 2) for t in range(n_tile)]

    def trade(even, odd, even_pairs, odd_pairs):
        swapped = lax.ppermute(odd, axes, [q for a, b in odd_pairs for q in ((a, b), (b, a))])
        gathered = lax.all_gather(even, axes, axis_index_groups=even_pairs)
        return gathered, swapped

    def trade_tiles(even, odd):
        return trade(even, odd, tile_even, tile_odd)

    def trade_secs(even, odd):
        return trade(even, odd, sec_even, sec_odd)

    u = displacement[0].reshape(2, 2, 32, LANES).transpose(0, 2, 1, 3).reshape(2, 64, LANES)
    c = stiffness[0].reshape(2, 32, LANES).transpose(1, 0, 2).reshape(64, LANES)
    off = match_offset[0]
    even, odd, own, ids, u, c = call(
        first_kernel,
        [((32, slots), F32), ((32, slots), F32), ((8, slots), F32), ((16, slots), jnp.int32), ((2, 64, LANES), F32), ((64, LANES), F32)],
        place, match_count, u, c, match_weight[0], off, source_row[0], source_col[0], target_row[0], target_col[0],
        scalars=2,
    )
    even_in, odd_in = trade_tiles(even, odd)
    even, odd = call(lambda *r: pack_kernel(True, *r), [((16, slots), F32)] * 2, place, even_in, odd_in, own)
    near, total = call(
        lambda *r: spring_kernel(True, *r), [((2, 64, LANES), F32), ((64, LANES), F32)], place, even_in, odd_in, u, c
    )
    sec_even_in, sec_odd_in = trade_secs(even, odd)
    u, share, even, odd, own_next = call(
        middle_kernel,
        [((2, 64, LANES), F32), ((64, LANES), F32), ((24, slots), F32), ((24, slots), F32), ((8, slots), F32)],
        place, sec_even_in, sec_odd_in, own, ids, off, u, c, near, total,
    )
    even_in, odd_in = trade_tiles(even, odd)
    even, odd = call(lambda *r: pack_kernel(False, *r), [((8, slots), F32)] * 2, place, even_in, odd_in, own_next)
    (near,) = call(lambda *r: spring_kernel(False, *r), [((2, 64, LANES), F32)], place, even_in, odd_in, u, c)
    sec_even_in, sec_odd_in = trade_secs(even, odd)
    (out,) = call(last_kernel, [((2, 64, LANES), F32)], place, sec_even_in, sec_odd_in, own, ids, off, u, near, share)
    return out.reshape(2, 32, 2, LANES).transpose(0, 2, 1, 3).reshape(1, 2, 2, 32 * LANES)


def solution(mesh):
    placed = (
        P("sec", None, "tile", None),
        P("sec", "tile", None),
        P("sec", "tile", None),
        P("sec", None, "tile", None),
        P("sec", "tile", None),
        P("sec", "tile", None),
        P("sec", "tile", None),
        P("sec", "tile", None),
        P("sec", "tile"),
    )

    def run(*args):
        return body(mesh.shape["sec"], mesh.shape["tile"], *args)

    return jax.shard_map(run, mesh=mesh, in_specs=placed, out_specs=P("sec", None, "tile", None), check_vma=False)
```

```python
import jax
import jax.numpy as jnp
from jax import lax
from jax.experimental import pallas as pl
from jax.experimental.pallas import tpu as pltpu
from jax.sharding import PartitionSpec as P

damping = 0.7
LANES = 128
F32 = jnp.float32
BF16 = jnp.bfloat16
HBM = pl.BlockSpec(memory_space=pltpu.HBM)
VMEM = pl.BlockSpec(memory_space=pltpu.VMEM)


def halves(value):
    high = value.astype(BF16)
    return high, (value - high.astype(F32)).astype(BF16)


def one_hot(index, depth):
    place = lax.broadcasted_iota(jnp.int32, (depth, index.shape[1]), 0)
    return place == index


def gather(table, lane_hot, block_mask):
    blocks = block_mask.shape[0]
    picked = jnp.dot(table, jnp.concatenate([lane_hot, lane_hot], axis=0), preferred_element_type=F32)
    return [
        jnp.sum(jnp.where(block_mask, picked[i * blocks : (i + 1) * blocks], 0.0), axis=0, keepdims=True)
        for i in range(picked.shape[0] // blocks)
    ]


def table_of(fields):
    high, low = halves(jnp.concatenate(fields, axis=0))
    return jnp.concatenate([high, low], axis=1)


def scatter(values, lane_hot, block_hot):
    parts = [halves(v) for v in values]
    left = jnp.concatenate([block_hot * p[k] for k in range(2) for p in parts], axis=0)
    return lax.dot_general(left, lane_hot, (((1,), (1,)), ((), ())), preferred_element_type=F32)


def wide(block):
    return jnp.concatenate([block[8 * i : 8 * i + 8] for i in range(4)], axis=1)


def narrow(rows):
    return jnp.concatenate([rows[:, LANES * i : LANES * (i + 1)] for i in range(4)], axis=0)


def side_sum(block):
    count = block.shape[0]
    lane = lax.broadcasted_iota(jnp.int32, block.shape, 1)
    row = lax.broadcasted_iota(jnp.int32, block.shape, 0)
    before = pltpu.roll(block, 1, 1)
    carried = jnp.where(row == 0, 0.0, pltpu.roll(before, 1, 0))
    before = jnp.where(lane == 0, carried, before)
    after = pltpu.roll(block, LANES - 1, 1)
    carried = jnp.where(row == count - 1, 0.0, pltpu.roll(after, count - 1, 0))
    after = jnp.where(lane == LANES - 1, carried, after)
    return before + after


def stencil(above, first, second, below):
    sides = [side_sum(b) for b in (above, first, second, below)]
    upper = first + 0.5 * sides[1]
    lower = second + 0.5 * sides[2]
    return jnp.concatenate(
        [
            above + 0.5 * sides[0] + lower + sides[1],
            upper + below + 0.5 * sides[3] + sides[2],
        ],
        axis=0,
    )


def rows_of(ref, lead=()):
    return [ref[lead + (pl.ds(r, 32, 2), slice(None))] for r in range(2)]


def fill(ref, rows):
    pad = (-len(rows)) % 8
    ref[...] = jnp.concatenate(rows + [jnp.zeros_like(rows[0])] * pad, axis=0)


def send_tiles(odd_tile, left, right, even_ref, odd_ref):
    even_ref[...] = jnp.where(odd_tile, left, right)
    odd_ref[...] = jnp.where(odd_tile, right, left)


def tile_message(halo, slot_rows):
    pad = (-len(slot_rows)) % 8
    rows = [wide(h) for h in halo] + slot_rows + [jnp.zeros_like(slot_rows[0])] * pad
    return jnp.concatenate(rows, axis=0)


def spot():
    return lax.axis_index("sec"), lax.axis_index("tile")


def first_kernel(n_sec, n_tile, *refs):
    far, (even_msg, odd_msg, own, ids, uo, co), held, sems = refs[:9], refs[9:15], refs[15:24], refs[24]
    copies = [pltpu.make_async_copy(f, h, sems.at[i]) for i, (f, h) in enumerate(zip(far, held))]
    for copy in copies:
        copy.start()
    for copy in copies:
        copy.wait()
    count, u, c, w, off, srow, scol, trow, tcol = held
    sec, tile = spot()
    field = [jnp.concatenate(rows_of(u, (i,)), axis=0) for i in range(2)]
    stiff = jnp.concatenate(rows_of(c), axis=0)
    for i in range(2):
        uo[i] = field[i]
    co[...] = stiff
    table = table_of(field)
    slot = lax.broadcasted_iota(jnp.int32, (1, w.shape[2]), 1)
    sources, targets, blocks, lanes, pulls = [], [], [], [], []
    for g in range(3):
        dest = tile + g - 1
        open_group = (sec < n_sec - 1) & (dest >= 0) & (dest < n_tile)
        limit = jnp.where(open_group, count[0:1, g : g + 1], 0)
        weight = jnp.where(slot < limit, w[g], 0.0)
        col = scol[g]
        block, lane = srow[g] * 32 + (col >> 7), col & 127
        blocks.append(block)
        lanes.append(lane)
        got = gather(table, one_hot(lane, LANES).astype(BF16), one_hot(block, 64))
        sources.append([weight * (got[i] - off[g, i : i + 1]) for i in range(2)] + [weight])
    for k in range(3):
        col = tcol[k]
        block, lane = trow[k] * 32 + (col >> 7), col & 127
        blocks.append(block)
        lanes.append(lane)
        targets.append(gather(table, one_hot(lane, LANES).astype(BF16), one_hot(block, 64)))
    halo = [stiff * field[0], stiff * field[1], stiff]
    left = tile_message([h[:32] for h in halo], sources[0] + targets[0])
    right = tile_message([h[32:] for h in halo], sources[2] + targets[2])
    send_tiles((tile & 1) == 1, left, right, even_msg, odd_msg)
    offsets = [off[g, i : i + 1] for g in range(3) for i in range(2)]
    fill(own, sources[1] + targets[1] + [s[2] for s in sources] + offsets)
    fill(ids, blocks + lanes)


def both_sides(even_in, odd_in, rows):
    parity = spot()[1] & 1
    even = even_in[1 - parity, rows, :]
    odd = odd_in[rows, :]
    return jnp.where(parity == 1, even, odd), jnp.where(parity == 1, odd, even)


def pack_kernel(first, even_in, odd_in, own, even_msg, odd_msg):
    base = 24 if first else 16
    n_src = 3 if first else 2
    left, right = both_sides(even_in, odd_in, slice(base, base + 8))
    own_rows = own[0:8]
    source = [m[i : i + 1] for m in (left, own_rows, right) for i in range(n_src)]
    target = [m[n_src + i : n_src + i + 1] for m in (left, own_rows, right) for i in range(2)]
    size = even_msg.shape[0]
    zero = jnp.zeros_like(source[0])
    source = jnp.concatenate(source + [zero] * (size - len(source)), axis=0)
    target = jnp.concatenate(target + [zero] * (size - len(target)), axis=0)
    send_tiles((spot()[0] & 1) == 1, target, source, even_msg, odd_msg)


def springs(fields, even_in, odd_in):
    up, down = both_sides(even_in, odd_in, slice(0, 8 * len(fields)))
    return [
        stencil(narrow(up[8 * i : 8 * i + 8]), f[:32], f[32:], narrow(down[8 * i : 8 * i + 8]))
        for i, f in enumerate(fields)
    ]


def arrivals(even_in, odd_in):
    parity = spot()[0] & 1
    even, odd = even_in[1 - parity], odd_in[parity]
    return jnp.where(parity == 1, even, odd), jnp.where(parity == 1, odd, even)


def offset_rows(own):
    return lambda g, i: own[8 + 2 * g + i : 9 + 2 * g + i, :]


def hots_of(ids):
    return [(one_hot(ids[6 + g : 7 + g], LANES).astype(BF16), one_hot(ids[g : g + 1], 64)) for g in range(6)]


def middle_kernel(
    even_tile, odd_tile, even_sec, odd_sec, own, ids, u, c, u_out, total_out, even_msg, odd_msg, own_out
):
    source_in, target_in = arrivals(even_sec, odd_sec)
    off = offset_rows(own)
    hots = hots_of(ids[...])
    weights = [own[5 + g : 6 + g, :] for g in range(3)]
    acc = jnp.zeros((384, LANES), F32)
    for g in range(6):
        if g < 3:
            vals = [weights[g] * (target_in[2 * g + i : 2 * g + i + 1] + off(g, i)) for i in range(2)] + [weights[g]]
        else:
            vals = [source_in[3 * (g - 3) + i : 3 * (g - 3) + i + 1] for i in range(3)]
        acc = acc + scatter(vals, hots[g][0], hots[g][1].astype(BF16))
    acc = acc[:192] + acc[192:]
    stiff = c[...]
    near = springs([stiff * u[0], stiff * u[1], stiff], even_tile, odd_tile)
    share = damping / (stiff * near[2] + acc[128:192])
    total_out[...] = share
    field = [(1.0 - damping) * u[i] + (stiff * near[i] + acc[64 * i : 64 * i + 64]) * share for i in range(2)]
    for i in range(2):
        u_out[i] = field[i]
    table = table_of(field)
    got = [gather(table, *h) for h in hots]
    sources = [[weights[g] * (got[g][i] - off(g, i)) for i in range(2)] for g in range(3)]
    targets = got[3:]
    halo = [stiff * field[0], stiff * field[1]]
    left = tile_message([h[:32] for h in halo], sources[0] + targets[0])
    right = tile_message([h[32:] for h in halo], sources[2] + targets[2])
    send_tiles((spot()[1] & 1) == 1, left, right, even_msg, odd_msg)
    fill(own_out, sources[1] + targets[1])


def last_kernel(even_tile, odd_tile, even_sec, odd_sec, own, ids, u, c, share, out):
    source_in, target_in = arrivals(even_sec, odd_sec)
    off = offset_rows(own)
    hots = hots_of(ids[...])
    acc = jnp.zeros((256, LANES), F32)
    for g in range(6):
        if g < 3:
            weight = own[5 + g : 6 + g, :]
            vals = [weight * (target_in[2 * g + i : 2 * g + i + 1] + off(g, i)) for i in range(2)]
        else:
            vals = [source_in[2 * (g - 3) + i : 2 * (g - 3) + i + 1] for i in range(2)]
        acc = acc + scatter(vals, hots[g][0], hots[g][1].astype(BF16))
    acc = acc[:128] + acc[128:]
    stiff = c[...]
    near = springs([stiff * u[0], stiff * u[1]], even_tile, odd_tile)
    for i in range(2):
        new = (1.0 - damping) * u[i] + (stiff * near[i] + acc[64 * i : 64 * i + 64]) * share[...]
        for r in range(2):
            out[i, pl.ds(r, 32, 2), :] = new[32 * r : 32 * r + 32]


def call(kernel, shapes, *args, held=False):
    scratch = [pltpu.VMEM(a.shape, a.dtype) for a in args] + [pltpu.SemaphoreType.DMA((len(args),))]
    return pl.pallas_call(
        kernel,
        out_shape=[jax.ShapeDtypeStruct(s, d) for s, d in shapes],
        in_specs=[HBM if held else VMEM] * len(args),
        out_specs=[VMEM] * len(shapes),
        scratch_shapes=scratch if held else [],
        compiler_params=pltpu.CompilerParams(vmem_limit_bytes=32 * 1024 * 1024),
    )(*([pltpu.with_memory_space_constraint(a, pltpu.HBM) for a in args] if held else args))


def body(n_sec, n_tile, displacement, stiffness, match_weight, match_offset, source_row, source_col, target_row, target_col, match_count):
    axes = ("sec", "tile")
    slots = match_weight.shape[2]

    def flat(s, t):
        return s % n_sec * n_tile + t

    tile_even = [[flat(s, t), flat(s, t + 1)] for s in range(n_sec) for t in range(0, n_tile, 2)]
    tile_odd = [[flat(s, t), flat(s, t + 1)] for s in range(n_sec) for t in range(1, n_tile - 1, 2)]
    sec_even = [[flat(s, t), flat(s + 1, t)] for s in range(0, n_sec, 2) for t in range(n_tile)]
    sec_odd = [[flat(s, t), flat(s + 1, t)] for s in range(1, n_sec, 2) for t in range(n_tile)]

    def trade_tiles(even, odd):
        swapped = lax.ppermute(odd, axes, [q for a, b in tile_odd for q in ((a, b), (b, a))])
        return lax.all_gather(even, axes, axis_index_groups=tile_even), swapped

    def trade_secs(even, odd):
        even_in = lax.all_gather(even, axes, axis_index_groups=sec_even)
        odd, even_in = lax.optimization_barrier((odd, even_in))
        return even_in, lax.all_gather(odd, axes, axis_index_groups=sec_odd)

    u = displacement[0].reshape(2, 2, 32, LANES).transpose(0, 2, 1, 3).reshape(2, 64, LANES)
    c = stiffness[0].reshape(2, 32, LANES).transpose(1, 0, 2).reshape(64, LANES)
    w, srow, scol, trow, tcol = [a.transpose(1, 0, 2) for a in (match_weight, source_row, source_col, target_row, target_col)]
    off = match_offset[0].transpose(1, 0, 2)
    even, odd, own, ids, u, c = call(
        lambda *r: first_kernel(n_sec, n_tile, *r),
        [((32, slots), F32), ((32, slots), F32), ((16, slots), F32), ((16, slots), jnp.int32), ((2, 64, LANES), F32), ((64, LANES), F32)],
        match_count, u, c, w, off, srow, scol, trow, tcol,
        held=True,
    )
    tiles_in = trade_tiles(even, odd)
    even, odd = call(lambda *r: pack_kernel(True, *r), [((16, slots), F32)] * 2, *tiles_in, own)
    u, share, even, odd, own_next = call(
        middle_kernel,
        [((2, 64, LANES), F32), ((64, LANES), F32), ((24, slots), F32), ((24, slots), F32), ((8, slots), F32)],
        *tiles_in, *trade_secs(even, odd), own, ids, u, c,
    )
    tiles_in = trade_tiles(even, odd)
    even, odd = call(lambda *r: pack_kernel(False, *r), [((8, slots), F32)] * 2, *tiles_in, own_next)
    (out,) = call(last_kernel, [((2, 64, LANES), F32)], *tiles_in, *trade_secs(even, odd), own, ids, u, c, share)
    return out.reshape(2, 32, 2, LANES).transpose(0, 2, 1, 3).reshape(1, 2, 2, 32 * LANES)


def solution(mesh):
    placed = (
        P("sec", None, "tile", None),
        P("sec", "tile", None),
        P("sec", "tile", None),
        P("sec", None, "tile", None),
        P("sec", "tile", None),
        P("sec", "tile", None),
        P("sec", "tile", None),
        P("sec", "tile", None),
        P("sec", "tile"),
    )

    def run(*args):
        return body(mesh.shape["sec"], mesh.shape["tile"], *args)

    return jax.shard_map(run, mesh=mesh, in_specs=placed, out_specs=P("sec", None, "tile", None), check_vma=False)
```

```python
import jax
import jax.numpy as jnp
from jax import lax
from jax.experimental import pallas as pl
from jax.experimental.pallas import tpu as pltpu
from jax.sharding import PartitionSpec as P

damping = 0.7
LANES = 128
F32 = jnp.float32
BF16 = jnp.bfloat16
HBM = pl.BlockSpec(memory_space=pltpu.HBM)
VMEM = pl.BlockSpec(memory_space=pltpu.VMEM)


def halves(value):
    high = value.astype(BF16)
    return high, (value - high.astype(F32)).astype(BF16)


def one_hot(index, depth):
    place = lax.broadcasted_iota(jnp.int32, (depth, index.shape[1]), 0)
    return place == index


def gather(table, lane_hot, block_mask):
    blocks = block_mask.shape[0]
    picked = jnp.dot(table, jnp.concatenate([lane_hot, lane_hot], axis=0), preferred_element_type=F32)
    return [
        jnp.sum(jnp.where(block_mask, picked[i * blocks : (i + 1) * blocks], 0.0), axis=0, keepdims=True)
        for i in range(picked.shape[0] // blocks)
    ]


def table_of(fields):
    high, low = halves(jnp.concatenate(fields, axis=0))
    return jnp.concatenate([high, low], axis=1)


def scatter(values, lane_hot, block_hot):
    parts = [halves(v) for v in values]
    left = jnp.concatenate([block_hot * p[k] for k in range(2) for p in parts], axis=0)
    return lax.dot_general(left, lane_hot, (((1,), (1,)), ((), ())), preferred_element_type=F32)


def wide(block):
    return jnp.concatenate([block[8 * i : 8 * i + 8] for i in range(4)], axis=1)


def narrow(rows):
    return jnp.concatenate([rows[:, LANES * i : LANES * (i + 1)] for i in range(4)], axis=0)


def side_sum(block):
    count = block.shape[0]
    lane = lax.broadcasted_iota(jnp.int32, block.shape, 1)
    row = lax.broadcasted_iota(jnp.int32, block.shape, 0)
    before = pltpu.roll(block, 1, 1)
    carried = jnp.where(row == 0, 0.0, pltpu.roll(before, 1, 0))
    before = jnp.where(lane == 0, carried, before)
    after = pltpu.roll(block, LANES - 1, 1)
    carried = jnp.where(row == count - 1, 0.0, pltpu.roll(after, count - 1, 0))
    after = jnp.where(lane == LANES - 1, carried, after)
    return before + after


def stencil(above, first, second, below):
    sides = [side_sum(b) for b in (above, first, second, below)]
    upper = first + 0.5 * sides[1]
    lower = second + 0.5 * sides[2]
    return jnp.concatenate(
        [
            above + 0.5 * sides[0] + lower + sides[1],
            upper + below + 0.5 * sides[3] + sides[2],
        ],
        axis=0,
    )


def rows_of(ref, lead=()):
    return [ref[lead + (pl.ds(r, 32, 2), slice(None))] for r in range(2)]


def fill(ref, rows):
    pad = (-len(rows)) % 8
    ref[...] = jnp.concatenate(rows + [jnp.zeros_like(rows[0])] * pad, axis=0)


def send_tiles(odd_tile, left, right, even_ref, odd_ref):
    even_ref[...] = jnp.where(odd_tile, left, right)
    odd_ref[...] = jnp.where(odd_tile, right, left)


def tile_message(halo, slot_rows):
    pad = (-len(slot_rows)) % 8
    rows = [wide(h) for h in halo] + slot_rows + [jnp.zeros_like(slot_rows[0])] * pad
    return jnp.concatenate(rows, axis=0)


def spot():
    return lax.axis_index("sec"), lax.axis_index("tile")


def first_kernel(n_sec, n_tile, *refs):
    far, (even_msg, odd_msg, own, ids, uo, co), held, sems = refs[:9], refs[9:15], refs[15:24], refs[24]
    copies = [pltpu.make_async_copy(f, h, sems.at[i]) for i, (f, h) in enumerate(zip(far, held))]
    for copy in copies:
        copy.start()
    for copy in copies:
        copy.wait()
    count, u, c, w, off, srow, scol, trow, tcol = held
    sec, tile = spot()
    field = [jnp.concatenate(rows_of(u, (i,)), axis=0) for i in range(2)]
    stiff = jnp.concatenate(rows_of(c), axis=0)
    for i in range(2):
        uo[i] = field[i]
    co[...] = stiff
    table = table_of(field)
    slot = lax.broadcasted_iota(jnp.int32, (1, w.shape[2]), 1)
    sources, targets, blocks, lanes, pulls = [], [], [], [], []
    for g in range(3):
        dest = tile + g - 1
        open_group = (sec < n_sec - 1) & (dest >= 0) & (dest < n_tile)
        limit = jnp.where(open_group, count[0:1, g : g + 1], 0)
        weight = jnp.where(slot < limit, w[g], 0.0)
        col = scol[g]
        block, lane = srow[g] * 32 + (col >> 7), col & 127
        blocks.append(block)
        lanes.append(lane)
        got = gather(table, one_hot(lane, LANES).astype(BF16), one_hot(block, 64))
        sources.append([weight * (got[i] - off[g, i : i + 1]) for i in range(2)] + [weight])
    for k in range(3):
        col = tcol[k]
        block, lane = trow[k] * 32 + (col >> 7), col & 127
        blocks.append(block)
        lanes.append(lane)
        targets.append(gather(table, one_hot(lane, LANES).astype(BF16), one_hot(block, 64)))
    send_secs(sources, targets, even_msg, odd_msg)
    offsets = [off[g, i : i + 1] for g in range(3) for i in range(2)]
    zero = jnp.zeros_like(offsets[0])
    fill(own, [zero] * 5 + [s[2] for s in sources] + offsets)
    fill(ids, blocks + lanes)


def send_secs(sources, targets, even_msg, odd_msg):
    size = even_msg.shape[0]
    source = [r for s in sources for r in s]
    target = [r for s in targets for r in s]
    zero = jnp.zeros_like(source[0])
    source = jnp.concatenate(source + [zero] * (size - len(source)), axis=0)
    target = jnp.concatenate(target + [zero] * (size - len(target)), axis=0)
    send_tiles((spot()[0] & 1) == 1, target, source, even_msg, odd_msg)


def both_sides(even_in, odd_in, rows):
    parity = spot()[1] & 1
    even = even_in[1 - parity, rows, :]
    odd = odd_in[rows, :]
    return jnp.where(parity == 1, even, odd), jnp.where(parity == 1, odd, even)


def pack_kernel(first, even_in, odd_in, u, c, even_msg, odd_msg, mid):
    n_src = 3 if first else 2
    source, target = arrivals(even_in, odd_in)
    rows = [
        [source[n_src * g + i : n_src * g + i + 1] for i in range(n_src)]
        + [target[2 * g + i : 2 * g + i + 1] for i in range(2)]
        for g in range(3)
    ]
    stiff = c[...]
    halo = [stiff * u[0], stiff * u[1]] + ([stiff] if first else [])
    left = tile_message([h[:32] for h in halo], rows[0])
    right = tile_message([h[32:] for h in halo], rows[2])
    send_tiles((spot()[1] & 1) == 1, left, right, even_msg, odd_msg)
    fill(mid, rows[1])


def slot_arrivals(first, even_in, odd_in, mid):
    base = 24 if first else 16
    n_src = 3 if first else 2
    left, right = both_sides(even_in, odd_in, slice(base, base + 8))
    sides = (left, mid[...], right)
    source = [m[i : i + 1] for m in sides for i in range(n_src)]
    target = [m[n_src + i : n_src + i + 1] for m in sides for i in range(2)]
    return source, target


def springs(fields, even_in, odd_in):
    up, down = both_sides(even_in, odd_in, slice(0, 8 * len(fields)))
    return [
        stencil(narrow(up[8 * i : 8 * i + 8]), f[:32], f[32:], narrow(down[8 * i : 8 * i + 8]))
        for i, f in enumerate(fields)
    ]


def arrivals(even_in, odd_in):
    sec = spot()[0]
    parity = sec & 1
    even, odd = even_in[1 - parity], odd_in[parity]
    source, target = jnp.where(parity == 1, even, odd), jnp.where(parity == 1, odd, even)
    return jnp.where(sec == 0, 0.0, source), target


def offset_rows(own):
    return lambda g, i: own[8 + 2 * g + i : 9 + 2 * g + i, :]


def hots_of(ids):
    return [(one_hot(ids[6 + g : 7 + g], LANES).astype(BF16), one_hot(ids[g : g + 1], 64)) for g in range(6)]


def middle_kernel(
    even_tile, odd_tile, mid, own, ids, u, c, u_out, total_out, even_msg, odd_msg
):
    source_in, target_in = slot_arrivals(True, even_tile, odd_tile, mid)
    off = offset_rows(own)
    hots = hots_of(ids[...])
    weights = [own[5 + g : 6 + g, :] for g in range(3)]
    acc = jnp.zeros((384, LANES), F32)
    for g in range(6):
        if g < 3:
            vals = [weights[g] * (target_in[2 * g + i] + off(g, i)) for i in range(2)] + [weights[g]]
        else:
            vals = [source_in[3 * (g - 3) + i] for i in range(3)]
        acc = acc + scatter(vals, hots[g][0], hots[g][1].astype(BF16))
    acc = acc[:192] + acc[192:]
    stiff = c[...]
    near = springs([stiff * u[0], stiff * u[1], stiff], even_tile, odd_tile)
    share = damping / (stiff * near[2] + acc[128:192])
    total_out[...] = share
    field = [(1.0 - damping) * u[i] + (stiff * near[i] + acc[64 * i : 64 * i + 64]) * share for i in range(2)]
    for i in range(2):
        u_out[i] = field[i]
    table = table_of(field)
    got = [gather(table, *h) for h in hots]
    sources = [[weights[g] * (got[g][i] - off(g, i)) for i in range(2)] for g in range(3)]
    send_secs(sources, got[3:], even_msg, odd_msg)


def last_kernel(even_tile, odd_tile, mid, own, ids, u, c, share, out):
    source_in, target_in = slot_arrivals(False, even_tile, odd_tile, mid)
    off = offset_rows(own)
    hots = hots_of(ids[...])
    acc = jnp.zeros((256, LANES), F32)
    for g in range(6):
        if g < 3:
            weight = own[5 + g : 6 + g, :]
            vals = [weight * (target_in[2 * g + i] + off(g, i)) for i in range(2)]
        else:
            vals = [source_in[2 * (g - 3) + i] for i in range(2)]
        acc = acc + scatter(vals, hots[g][0], hots[g][1].astype(BF16))
    acc = acc[:128] + acc[128:]
    stiff = c[...]
    near = springs([stiff * u[0], stiff * u[1]], even_tile, odd_tile)
    for i in range(2):
        new = (1.0 - damping) * u[i] + (stiff * near[i] + acc[64 * i : 64 * i + 64]) * share[...]
        for r in range(2):
            out[i, pl.ds(r, 32, 2), :] = new[32 * r : 32 * r + 32]


def call(kernel, shapes, *args, held=False):
    scratch = [pltpu.VMEM(a.shape, a.dtype) for a in args] + [pltpu.SemaphoreType.DMA((len(args),))]
    return pl.pallas_call(
        kernel,
        out_shape=[jax.ShapeDtypeStruct(s, d) for s, d in shapes],
        in_specs=[HBM if held else VMEM] * len(args),
        out_specs=[VMEM] * len(shapes),
        scratch_shapes=scratch if held else [],
        compiler_params=pltpu.CompilerParams(vmem_limit_bytes=32 * 1024 * 1024),
    )(*([pltpu.with_memory_space_constraint(a, pltpu.HBM) for a in args] if held else args))


def body(n_sec, n_tile, displacement, stiffness, match_weight, match_offset, source_row, source_col, target_row, target_col, match_count):
    axes = ("sec", "tile")
    slots = match_weight.shape[2]

    def flat(s, t):
        return s % n_sec * n_tile + t

    tile_even = [[flat(s, t), flat(s, t + 1)] for s in range(n_sec) for t in range(0, n_tile, 2)]
    tile_odd = [[flat(s, t), flat(s, t + 1)] for s in range(n_sec) for t in range(1, n_tile - 1, 2)]
    sec_even = [[flat(s, t), flat(s + 1, t)] for s in range(0, n_sec, 2) for t in range(n_tile)]
    sec_odd = [[flat(s, t), flat(s + 1, t)] for s in range(1, n_sec - 1, 2) for t in range(n_tile)]
    sec_odd += [[flat(s, t), flat(s, t + 1)] for s in (0, n_sec - 1) for t in range(0, n_tile, 2)]

    def trade_tiles(even, odd):
        swapped = lax.ppermute(odd, axes, [q for a, b in tile_odd for q in ((a, b), (b, a))])
        return lax.all_gather(even, axes, axis_index_groups=tile_even), swapped

    def trade_secs(even, odd):
        even_in = lax.all_gather(even, axes, axis_index_groups=sec_even)
        odd, even_in = lax.optimization_barrier((odd, even_in))
        return even_in, lax.all_gather(odd, axes, axis_index_groups=sec_odd)

    u = displacement[0].reshape(2, 2, 32, LANES).transpose(0, 2, 1, 3).reshape(2, 64, LANES)
    c = stiffness[0].reshape(2, 32, LANES).transpose(1, 0, 2).reshape(64, LANES)
    w, srow, scol, trow, tcol = [a.transpose(1, 0, 2) for a in (match_weight, source_row, source_col, target_row, target_col)]
    off = match_offset[0].transpose(1, 0, 2)
    even, odd, own, ids, u, c = call(
        lambda *r: first_kernel(n_sec, n_tile, *r),
        [((16, slots), F32), ((16, slots), F32), ((16, slots), F32), ((16, slots), jnp.int32), ((2, 64, LANES), F32), ((64, LANES), F32)],
        match_count, u, c, w, off, srow, scol, trow, tcol,
        held=True,
    )
    even, odd, mid = call(
        lambda *r: pack_kernel(True, *r), [((32, slots), F32)] * 2 + [((8, slots), F32)], *trade_secs(even, odd), u, c
    )
    u, share, even, odd = call(
        middle_kernel,
        [((2, 64, LANES), F32), ((64, LANES), F32), ((8, slots), F32), ((8, slots), F32)],
        *trade_tiles(even, odd), mid, own, ids, u, c,
    )
    even, odd, mid = call(
        lambda *r: pack_kernel(False, *r), [((24, slots), F32)] * 2 + [((8, slots), F32)], *trade_secs(even, odd), u, c
    )
    (out,) = call(last_kernel, [((2, 64, LANES), F32)], *trade_tiles(even, odd), mid, own, ids, u, c, share)
    return out.reshape(2, 32, 2, LANES).transpose(0, 2, 1, 3).reshape(1, 2, 2, 32 * LANES)


def solution(mesh):
    placed = (
        P("sec", None, "tile", None),
        P("sec", "tile", None),
        P("sec", "tile", None),
        P("sec", None, "tile", None),
        P("sec", "tile", None),
        P("sec", "tile", None),
        P("sec", "tile", None),
        P("sec", "tile", None),
        P("sec", "tile"),
    )

    def run(*args):
        return body(mesh.shape["sec"], mesh.shape["tile"], *args)

    return jax.shard_map(run, mesh=mesh, in_specs=placed, out_specs=P("sec", None, "tile", None), check_vma=False)
```

```python
import jax
import jax.numpy as jnp
from jax import lax
from jax.experimental import pallas as pl
from jax.experimental.pallas import tpu as pltpu
from jax.sharding import PartitionSpec as P

damping = 0.7
LANES = 128
F32 = jnp.float32
BF16 = jnp.bfloat16
HBM = pl.BlockSpec(memory_space=pltpu.HBM)
VMEM = pl.BlockSpec(memory_space=pltpu.VMEM)


def halves(value):
    high = value.astype(BF16)
    return high, (value - high.astype(F32)).astype(BF16)


def one_hot(index, depth):
    place = lax.broadcasted_iota(jnp.int32, (depth, index.shape[1]), 0)
    return place == index


def lane_one_hot(lane):
    place = lax.broadcasted_iota(jnp.int32, (LANES, LANES), 0).astype(BF16)
    place = jnp.concatenate([place] * (lane.shape[1] // LANES), axis=1)
    return jnp.where(place == lane.astype(BF16), jnp.bfloat16(1), jnp.bfloat16(0))


def wide_rows(rows):
    return jnp.concatenate(rows, axis=1)


def gather(fields, lane_hot, block_mask):
    high, low = halves(jnp.concatenate(fields, axis=0))
    table = jnp.concatenate([high, low], axis=1)
    picked = jnp.dot(table, jnp.concatenate([lane_hot, lane_hot], axis=0), preferred_element_type=F32)
    blocks = block_mask.shape[0]
    return [
        jnp.sum(jnp.where(block_mask, picked[i * blocks : (i + 1) * blocks], 0.0), axis=0, keepdims=True)
        for i in range(len(fields))
    ]


def scatter(values, lane_hot, block_hot):
    parts = [halves(v) for v in values]
    left = jnp.concatenate([block_hot * p[k] for k in range(2) for p in parts], axis=0)
    total = lax.dot_general(left, lane_hot, (((1,), (1,)), ((), ())), preferred_element_type=F32)
    return total[: total.shape[0] // 2] + total[total.shape[0] // 2 :]


def cut(rows):
    pieces = [row[:, LANES * i : LANES * (i + 1)] for row in rows for i in range(row.shape[1] // LANES)]
    return pieces + [jnp.zeros_like(pieces[0])] * ((-len(pieces)) % 8)


def slot_row(block, place):
    return jnp.concatenate([block[4 * place + i : 4 * place + i + 1] for i in range(4)], axis=1)


def side_sum(block):
    count = block.shape[0]
    lane = lax.broadcasted_iota(jnp.int32, block.shape, 1)
    row = lax.broadcasted_iota(jnp.int32, block.shape, 0)
    before = pltpu.roll(block, 1, 1)
    carried = jnp.where(row == 0, 0.0, pltpu.roll(before, 1, 0))
    before = jnp.where(lane == 0, carried, before)
    after = pltpu.roll(block, LANES - 1, 1)
    carried = jnp.where(row == count - 1, 0.0, pltpu.roll(after, count - 1, 0))
    after = jnp.where(lane == LANES - 1, carried, after)
    return before + after


def stencil(above, first, second, below):
    sides = [side_sum(b) for b in (above, first, second, below)]
    upper = first + 0.5 * sides[1]
    lower = second + 0.5 * sides[2]
    return jnp.concatenate(
        [
            above + 0.5 * sides[0] + lower + sides[1],
            upper + below + 0.5 * sides[3] + sides[2],
        ],
        axis=0,
    )


def rows_of(ref, lead=()):
    return [ref[lead + (pl.ds(r, 32, 2), slice(None))] for r in range(2)]


def fill(ref, rows):
    pad = (-len(rows)) % 8
    ref[...] = jnp.concatenate(rows + [jnp.zeros_like(rows[0])] * pad, axis=0)


def send_tiles(odd_tile, left, right, even_ref, odd_ref):
    even_ref[...] = jnp.where(odd_tile, left, right)
    odd_ref[...] = jnp.where(odd_tile, right, left)


def tile_message(halo, slot_rows):
    return jnp.concatenate(halo + cut(slot_rows), axis=0)


def spot():
    return lax.axis_index("sec"), lax.axis_index("tile")


def first_kernel(n_sec, n_tile, *refs):
    far, (even_msg, odd_msg, own, ids, uo, co), held, sems = refs[:9], refs[9:15], refs[15:24], refs[24]
    copies = [pltpu.make_async_copy(f, h, sems.at[i]) for i, (f, h) in enumerate(zip(far, held))]
    for copy in copies:
        copy.start()
    for copy in copies:
        copy.wait()
    count, u, c, w, off, srow, scol, trow, tcol = held
    sec, tile = spot()
    field = [jnp.concatenate(rows_of(u, (i,)), axis=0) for i in range(2)]
    stiff = jnp.concatenate(rows_of(c), axis=0)
    for i in range(2):
        uo[i] = field[i]
    co[...] = stiff
    slot = lax.broadcasted_iota(jnp.int32, (1, w.shape[2]), 1)
    rows = [(srow, scol, g) for g in range(3)] + [(trow, tcol, k) for k in range(3)]
    blocks = [row[g] * 32 + (col[g] >> 7) for row, col, g in rows]
    lanes = [col[g] & 127 for row, col, g in rows]
    got = gather(field, lane_one_hot(wide_rows(lanes)), one_hot(wide_rows(blocks), 64))
    got = [[v[:, slot.shape[1] * g : slot.shape[1] * (g + 1)] for v in got] for g in range(6)]
    sources = []
    for g in range(3):
        dest = tile + g - 1
        open_group = (sec < n_sec - 1) & (dest >= 0) & (dest < n_tile)
        limit = jnp.where(open_group, count[0:1, g : g + 1], 0)
        weight = jnp.where(slot < limit, w[g], 0.0)
        sources.append([weight * (got[g][i] - off[g, i : i + 1]) for i in range(2)] + [weight])
    targets = got[3:]
    send_secs(sources, targets, even_msg, odd_msg)
    offsets = [off[g, i : i + 1] for g in range(3) for i in range(2)]
    zero = jnp.zeros_like(offsets[0])
    fill(own, [zero] * 5 + [s[2] for s in sources] + offsets)
    fill(ids, blocks + lanes)


def send_secs(sources, targets, even_msg, odd_msg):
    size = even_msg.shape[0]
    source = cut([r for s in sources for r in s])
    target = cut([r for s in targets for r in s])
    zero = jnp.zeros_like(source[0])
    source = jnp.concatenate(source + [zero] * (size - len(source)), axis=0)
    target = jnp.concatenate(target + [zero] * (size - len(target)), axis=0)
    send_tiles((spot()[0] & 1) == 1, target, source, even_msg, odd_msg)


def both_sides(even_in, odd_in, rows):
    parity = spot()[1] & 1
    even = even_in[1 - parity, rows, :]
    odd = odd_in[rows, :]
    return jnp.where(parity == 1, even, odd), jnp.where(parity == 1, odd, even)


def pack_kernel(first, even_in, odd_in, u, c, even_msg, odd_msg, mid):
    n_src = 3 if first else 2
    source, target = arrivals(even_in, odd_in)
    rows = [
        [slot_row(source, n_src * g + i) for i in range(n_src)] + [slot_row(target, 2 * g + i) for i in range(2)]
        for g in range(3)
    ]
    stiff = c[...]
    halo = [stiff * u[0], stiff * u[1]] + ([stiff] if first else [])
    left = tile_message([h[:32] for h in halo], rows[0])
    right = tile_message([h[32:] for h in halo], rows[2])
    send_tiles((spot()[1] & 1) == 1, left, right, even_msg, odd_msg)
    fill(mid, rows[1])


def slot_arrivals(first, even_in, odd_in, mid):
    base = 96 if first else 64
    n_src = 3 if first else 2
    left, right = both_sides(even_in, odd_in, slice(base, even_in.shape[1]))
    sides = [[slot_row(m, i) for i in range(n_src + 2)] for m in (left, right)]
    sides.insert(1, [mid[i : i + 1, :] for i in range(n_src + 2)])
    source = [m[i] for m in sides for i in range(n_src)]
    target = [m[n_src + i] for m in sides for i in range(2)]
    return source, target


def springs(fields, even_in, odd_in):
    up, down = both_sides(even_in, odd_in, slice(0, 32 * len(fields)))
    return [
        stencil(up[32 * i : 32 * i + 32], f[:32], f[32:], down[32 * i : 32 * i + 32])
        for i, f in enumerate(fields)
    ]


def arrivals(even_in, odd_in):
    sec = spot()[0]
    parity = sec & 1
    even, odd = even_in[1 - parity], odd_in[parity]
    source, target = jnp.where(parity == 1, even, odd), jnp.where(parity == 1, odd, even)
    return jnp.where(sec == 0, 0.0, source), target


def offset_rows(own):
    return lambda g, i: own[8 + 2 * g + i : 9 + 2 * g + i, :]


def hots_of(ids):
    lane = wide_rows([ids[6 + g : 7 + g] for g in range(6)])
    block = wide_rows([ids[g : g + 1] for g in range(6)])
    return lane_one_hot(lane), one_hot(block, 64)


def middle_kernel(even_tile, odd_tile, mid, own, ids, u, c, u_out, total_out, even_msg, odd_msg):
    source_in, target_in = slot_arrivals(True, even_tile, odd_tile, mid)
    off = offset_rows(own)
    lane_hot, block_mask = hots_of(ids[...])
    weights = [own[5 + g : 6 + g, :] for g in range(3)]
    values = [
        wide_rows([weights[g] * (target_in[2 * g + i] + off(g, i)) for g in range(3)] + [source_in[3 * k + i] for k in range(3)])
        for i in range(2)
    ]
    values.append(wide_rows(weights + [source_in[3 * k + 2] for k in range(3)]))
    acc = scatter(values, lane_hot, block_mask.astype(BF16))
    stiff = c[...]
    near = springs([stiff * u[0], stiff * u[1], stiff], even_tile, odd_tile)
    share = damping / (stiff * near[2] + acc[128:192])
    total_out[...] = share
    field = [(1.0 - damping) * u[i] + (stiff * near[i] + acc[64 * i : 64 * i + 64]) * share for i in range(2)]
    for i in range(2):
        u_out[i] = field[i]
    got = gather(field, lane_hot, block_mask)
    size = weights[0].shape[1]
    got = [[v[:, size * g : size * (g + 1)] for v in got] for g in range(6)]
    sources = [[weights[g] * (got[g][i] - off(g, i)) for i in range(2)] for g in range(3)]
    send_secs(sources, got[3:], even_msg, odd_msg)


def last_kernel(even_tile, odd_tile, mid, own, ids, u, c, share, out):
    source_in, target_in = slot_arrivals(False, even_tile, odd_tile, mid)
    off = offset_rows(own)
    lane_hot, block_mask = hots_of(ids[...])
    weights = [own[5 + g : 6 + g, :] for g in range(3)]
    values = [
        wide_rows([weights[g] * (target_in[2 * g + i] + off(g, i)) for g in range(3)] + [source_in[2 * k + i] for k in range(3)])
        for i in range(2)
    ]
    acc = scatter(values, lane_hot, block_mask.astype(BF16))
    stiff = c[...]
    near = springs([stiff * u[0], stiff * u[1]], even_tile, odd_tile)
    for i in range(2):
        new = (1.0 - damping) * u[i] + (stiff * near[i] + acc[64 * i : 64 * i + 64]) * share[...]
        for r in range(2):
            out[i, pl.ds(r, 32, 2), :] = new[32 * r : 32 * r + 32]


def call(kernel, shapes, *args, held=False):
    scratch = [pltpu.VMEM(a.shape, a.dtype) for a in args] + [pltpu.SemaphoreType.DMA((len(args),))]
    return pl.pallas_call(
        kernel,
        out_shape=[jax.ShapeDtypeStruct(s, d) for s, d in shapes],
        in_specs=[HBM if held else VMEM] * len(args),
        out_specs=[VMEM] * len(shapes),
        scratch_shapes=scratch if held else [],
        compiler_params=pltpu.CompilerParams(vmem_limit_bytes=32 * 1024 * 1024),
    )(*([pltpu.with_memory_space_constraint(a, pltpu.HBM) for a in args] if held else args))


def body(n_sec, n_tile, displacement, stiffness, match_weight, match_offset, source_row, source_col, target_row, target_col, match_count):
    axes = ("sec", "tile")
    slots = match_weight.shape[2]

    def flat(s, t):
        return s % n_sec * n_tile + t

    tile_even = [[flat(s, t), flat(s, t + 1)] for s in range(n_sec) for t in range(0, n_tile, 2)]
    tile_odd = [[flat(s, t), flat(s, t + 1)] for s in range(n_sec) for t in range(1, n_tile - 1, 2)]
    sec_even = [[flat(s, t), flat(s + 1, t)] for s in range(0, n_sec, 2) for t in range(n_tile)]
    sec_odd = [[flat(s, t), flat(s + 1, t)] for s in range(1, n_sec - 1, 2) for t in range(n_tile)]
    sec_odd += [[flat(s, t), flat(s, t + 1)] for s in (0, n_sec - 1) for t in range(0, n_tile, 2)]

    def trade_tiles(even, odd):
        swapped = lax.ppermute(odd, axes, [q for a, b in tile_odd for q in ((a, b), (b, a))])
        return lax.all_gather(even, axes, axis_index_groups=tile_even), swapped

    def trade_secs(even, odd):
        even_in = lax.all_gather(even, axes, axis_index_groups=sec_even)
        odd, even_in = lax.optimization_barrier((odd, even_in))
        return even_in, lax.all_gather(odd, axes, axis_index_groups=sec_odd)

    u = displacement[0].reshape(2, 2, 32, LANES).transpose(0, 2, 1, 3).reshape(2, 64, LANES)
    c = stiffness[0].reshape(2, 32, LANES).transpose(1, 0, 2).reshape(64, LANES)
    w, srow, scol, trow, tcol = [a.transpose(1, 0, 2) for a in (match_weight, source_row, source_col, target_row, target_col)]
    off = match_offset[0].transpose(1, 0, 2)
    even, odd, own, ids, u, c = call(
        lambda *r: first_kernel(n_sec, n_tile, *r),
        [((40, LANES), F32), ((40, LANES), F32), ((16, slots), F32), ((16, slots), jnp.int32), ((2, 64, LANES), F32), ((64, LANES), F32)],
        match_count, u, c, w, off, srow, scol, trow, tcol,
        held=True,
    )
    even, odd, mid = call(
        lambda *r: pack_kernel(True, *r), [((120, LANES), F32)] * 2 + [((8, slots), F32)], *trade_secs(even, odd), u, c
    )
    u, share, even, odd = call(
        middle_kernel,
        [((2, 64, LANES), F32), ((64, LANES), F32), ((24, LANES), F32), ((24, LANES), F32)],
        *trade_tiles(even, odd), mid, own, ids, u, c,
    )
    even, odd, mid = call(
        lambda *r: pack_kernel(False, *r), [((80, LANES), F32)] * 2 + [((8, slots), F32)], *trade_secs(even, odd), u, c
    )
    (out,) = call(last_kernel, [((2, 64, LANES), F32)], *trade_tiles(even, odd), mid, own, ids, u, c, share)
    return out.reshape(2, 32, 2, LANES).transpose(0, 2, 1, 3).reshape(1, 2, 2, 32 * LANES)


def solution(mesh):
    placed = (
        P("sec", None, "tile", None),
        P("sec", "tile", None),
        P("sec", "tile", None),
        P("sec", None, "tile", None),
        P("sec", "tile", None),
        P("sec", "tile", None),
        P("sec", "tile", None),
        P("sec", "tile", None),
        P("sec", "tile"),
    )

    def run(*args):
        return body(mesh.shape["sec"], mesh.shape["tile"], *args)

    return jax.shard_map(run, mesh=mesh, in_specs=placed, out_specs=P("sec", None, "tile", None), check_vma=False)
```

```python
import jax
import jax.numpy as jnp
from jax import lax
from jax.experimental import pallas as pl
from jax.experimental.pallas import tpu as pltpu
from jax.sharding import PartitionSpec as P

damping = 0.7
LANES = 128
F32 = jnp.float32
BF16 = jnp.bfloat16
HBM = pl.BlockSpec(memory_space=pltpu.HBM)
VMEM = pl.BlockSpec(memory_space=pltpu.VMEM)


def halves(value):
    high = value.astype(BF16)
    return high, (value - high.astype(F32)).astype(BF16)


def one_hot(index, depth):
    place = lax.broadcasted_iota(jnp.int32, (depth, index.shape[1]), 0)
    return place == index


def lane_one_hot(lane):
    place = lax.broadcasted_iota(jnp.int32, (LANES, LANES), 0).astype(BF16)
    place = jnp.concatenate([place] * (lane.shape[1] // LANES), axis=1)
    return jnp.where(place == lane.astype(BF16), jnp.bfloat16(1), jnp.bfloat16(0))


def wide_rows(rows):
    return jnp.concatenate(rows, axis=1)


def gather(fields, lane_hot, block_mask):
    high, low = halves(jnp.concatenate(fields, axis=0))
    table = jnp.concatenate([high, low], axis=1)
    picked = jnp.dot(table, jnp.concatenate([lane_hot, lane_hot], axis=0), preferred_element_type=F32)
    blocks = block_mask.shape[0]
    return [
        jnp.sum(jnp.where(block_mask, picked[i * blocks : (i + 1) * blocks], 0.0), axis=0, keepdims=True)
        for i in range(len(fields))
    ]


def scatter(values, lane_hot, block_hot):
    left = jnp.concatenate([block_hot * v.astype(BF16) for v in values], axis=0)
    return lax.dot_general(left, lane_hot, (((1,), (1,)), ((), ())), preferred_element_type=F32)


def cut(rows):
    pieces = [row[:, LANES * i : LANES * (i + 1)] for row in rows for i in range(row.shape[1] // LANES)]
    return pieces + [jnp.zeros_like(pieces[0])] * ((-len(pieces)) % 8)


def slot_row(block, place):
    return jnp.concatenate([block[4 * place + i : 4 * place + i + 1] for i in range(4)], axis=1)


def side_sum(block):
    count = block.shape[0]
    lane = lax.broadcasted_iota(jnp.int32, block.shape, 1)
    row = lax.broadcasted_iota(jnp.int32, block.shape, 0)
    before = pltpu.roll(block, 1, 1)
    carried = jnp.where(row == 0, 0.0, pltpu.roll(before, 1, 0))
    before = jnp.where(lane == 0, carried, before)
    after = pltpu.roll(block, LANES - 1, 1)
    carried = jnp.where(row == count - 1, 0.0, pltpu.roll(after, count - 1, 0))
    after = jnp.where(lane == LANES - 1, carried, after)
    return before + after


def stencil(above, first, second, below):
    sides = [side_sum(b) for b in (above, first, second, below)]
    upper = first + 0.5 * sides[1]
    lower = second + 0.5 * sides[2]
    return jnp.concatenate(
        [
            above + 0.5 * sides[0] + lower + sides[1],
            upper + below + 0.5 * sides[3] + sides[2],
        ],
        axis=0,
    )


def rows_of(ref, lead=()):
    return [ref[lead + (pl.ds(r, 32, 2), slice(None))] for r in range(2)]


def fill(ref, rows):
    pad = (-len(rows)) % 8
    ref[...] = jnp.concatenate(rows + [jnp.zeros_like(rows[0])] * pad, axis=0)


def send_tiles(odd_tile, left, right, even_ref, odd_ref):
    even_ref[...] = jnp.where(odd_tile, left, right)
    odd_ref[...] = jnp.where(odd_tile, right, left)


def tile_message(halo, slot_rows):
    return jnp.concatenate(halo + cut(slot_rows), axis=0)


def spot():
    return lax.axis_index("sec"), lax.axis_index("tile")


def first_kernel(n_sec, n_tile, *refs):
    far, (even_msg, odd_msg, own, ids, uo, co), held, sems = refs[:9], refs[9:15], refs[15:24], refs[24]
    copies = [pltpu.make_async_copy(f, h, sems.at[i]) for i, (f, h) in enumerate(zip(far, held))]
    for copy in copies:
        copy.start()
    for copy in copies:
        copy.wait()
    count, u, c, w, off, srow, scol, trow, tcol = held
    sec, tile = spot()
    field = [jnp.concatenate(rows_of(u, (i,)), axis=0) for i in range(2)]
    stiff = jnp.concatenate(rows_of(c), axis=0)
    for i in range(2):
        uo[i] = field[i]
    co[...] = stiff
    slot = lax.broadcasted_iota(jnp.int32, (1, w.shape[2]), 1)
    rows = [(srow, scol, g) for g in range(3)] + [(trow, tcol, k) for k in range(3)]
    blocks = [row[g] * 32 + (col[g] >> 7) for row, col, g in rows]
    lanes = [col[g] & 127 for row, col, g in rows]
    got = gather(field, lane_one_hot(wide_rows(lanes)), one_hot(wide_rows(blocks), 64))
    got = [[v[:, slot.shape[1] * g : slot.shape[1] * (g + 1)] for v in got] for g in range(6)]
    sources = []
    for g in range(3):
        dest = tile + g - 1
        open_group = (sec < n_sec - 1) & (dest >= 0) & (dest < n_tile)
        limit = jnp.where(open_group, count[0:1, g : g + 1], 0)
        weight = jnp.where(slot < limit, w[g], 0.0)
        sources.append([weight * (got[g][i] - off[g, i : i + 1]) for i in range(2)] + [weight])
    targets = got[3:]
    send_secs(sources, targets, even_msg, odd_msg)
    offsets = [off[g, i : i + 1] for g in range(3) for i in range(2)]
    zero = jnp.zeros_like(offsets[0])
    fill(own, [zero] * 5 + [s[2] for s in sources] + offsets)
    fill(ids, blocks + lanes)


def send_secs(sources, targets, even_msg, odd_msg):
    size = even_msg.shape[0]
    source = cut([r for s in sources for r in s])
    target = cut([r for s in targets for r in s])
    zero = jnp.zeros_like(source[0])
    source = jnp.concatenate(source + [zero] * (size - len(source)), axis=0)
    target = jnp.concatenate(target + [zero] * (size - len(target)), axis=0)
    send_tiles((spot()[0] & 1) == 1, target, source, even_msg, odd_msg)


def both_sides(even_in, odd_in, rows):
    parity = spot()[1] & 1
    even = even_in[1 - parity, rows, :]
    odd = odd_in[rows, :]
    return jnp.where(parity == 1, even, odd), jnp.where(parity == 1, odd, even)


def pack_kernel(first, even_in, odd_in, u, c, even_msg, odd_msg, mid):
    n_src = 3 if first else 2
    source, target = arrivals(even_in, odd_in)
    rows = [
        [slot_row(source, n_src * g + i) for i in range(n_src)] + [slot_row(target, 2 * g + i) for i in range(2)]
        for g in range(3)
    ]
    stiff = c[...]
    halo = [stiff * u[0], stiff * u[1]] + ([stiff] if first else [])
    left = tile_message([h[:32] for h in halo], rows[0])
    right = tile_message([h[32:] for h in halo], rows[2])
    send_tiles((spot()[1] & 1) == 1, left, right, even_msg, odd_msg)
    fill(mid, rows[1])


def slot_arrivals(first, even_in, odd_in, mid):
    base = 96 if first else 64
    n_src = 3 if first else 2
    left, right = both_sides(even_in, odd_in, slice(base, even_in.shape[1]))
    sides = [[slot_row(m, i) for i in range(n_src + 2)] for m in (left, right)]
    sides.insert(1, [mid[i : i + 1, :] for i in range(n_src + 2)])
    source = [m[i] for m in sides for i in range(n_src)]
    target = [m[n_src + i] for m in sides for i in range(2)]
    return source, target


def springs(fields, even_in, odd_in):
    up, down = both_sides(even_in, odd_in, slice(0, 32 * len(fields)))
    return [
        stencil(up[32 * i : 32 * i + 32], f[:32], f[32:], down[32 * i : 32 * i + 32])
        for i, f in enumerate(fields)
    ]


def arrivals(even_in, odd_in):
    sec = spot()[0]
    parity = sec & 1
    even, odd = even_in[1 - parity], odd_in[parity]
    source, target = jnp.where(parity == 1, even, odd), jnp.where(parity == 1, odd, even)
    return jnp.where(sec == 0, 0.0, source), target


def offset_rows(own):
    return lambda g, i: own[8 + 2 * g + i : 9 + 2 * g + i, :]


def hots_of(ids):
    lane = wide_rows([ids[6 + g : 7 + g] for g in range(6)])
    block = wide_rows([ids[g : g + 1] for g in range(6)])
    return lane_one_hot(lane), one_hot(block, 64)


def middle_kernel(even_tile, odd_tile, mid, own, ids, u, c, u_out, total_out, even_msg, odd_msg):
    source_in, target_in = slot_arrivals(True, even_tile, odd_tile, mid)
    off = offset_rows(own)
    lane_hot, block_mask = hots_of(ids[...])
    weights = [own[5 + g : 6 + g, :] for g in range(3)]
    values = [
        wide_rows([weights[g] * (target_in[2 * g + i] + off(g, i)) for g in range(3)] + [source_in[3 * k + i] for k in range(3)])
        for i in range(2)
    ]
    values.append(wide_rows(weights + [source_in[3 * k + 2] for k in range(3)]))
    acc = scatter(values, lane_hot, block_mask.astype(BF16))
    stiff = c[...]
    near = springs([stiff * u[0], stiff * u[1], stiff], even_tile, odd_tile)
    share = damping / (stiff * near[2] + acc[128:192])
    total_out[...] = share
    field = [(1.0 - damping) * u[i] + (stiff * near[i] + acc[64 * i : 64 * i + 64]) * share for i in range(2)]
    for i in range(2):
        u_out[i] = field[i]
    got = gather(field, lane_hot, block_mask)
    size = weights[0].shape[1]
    got = [[v[:, size * g : size * (g + 1)] for v in got] for g in range(6)]
    sources = [[weights[g] * (got[g][i] - off(g, i)) for i in range(2)] for g in range(3)]
    send_secs(sources, got[3:], even_msg, odd_msg)


def last_kernel(even_tile, odd_tile, mid, own, ids, u, c, share, out):
    source_in, target_in = slot_arrivals(False, even_tile, odd_tile, mid)
    off = offset_rows(own)
    lane_hot, block_mask = hots_of(ids[...])
    weights = [own[5 + g : 6 + g, :] for g in range(3)]
    values = [
        wide_rows([weights[g] * (target_in[2 * g + i] + off(g, i)) for g in range(3)] + [source_in[2 * k + i] for k in range(3)])
        for i in range(2)
    ]
    acc = scatter(values, lane_hot, block_mask.astype(BF16))
    stiff = c[...]
    near = springs([stiff * u[0], stiff * u[1]], even_tile, odd_tile)
    for i in range(2):
        new = (1.0 - damping) * u[i] + (stiff * near[i] + acc[64 * i : 64 * i + 64]) * share[...]
        for r in range(2):
            out[i, pl.ds(r, 32, 2), :] = new[32 * r : 32 * r + 32]


def call(kernel, shapes, *args, held=False):
    scratch = [pltpu.VMEM(a.shape, a.dtype) for a in args] + [pltpu.SemaphoreType.DMA((len(args),))]
    return pl.pallas_call(
        kernel,
        out_shape=[jax.ShapeDtypeStruct(s, d) for s, d in shapes],
        in_specs=[HBM if held else VMEM] * len(args),
        out_specs=[VMEM] * len(shapes),
        scratch_shapes=scratch if held else [],
        compiler_params=pltpu.CompilerParams(vmem_limit_bytes=32 * 1024 * 1024),
    )(*([pltpu.with_memory_space_constraint(a, pltpu.HBM) for a in args] if held else args))


def body(n_sec, n_tile, displacement, stiffness, match_weight, match_offset, source_row, source_col, target_row, target_col, match_count):
    axes = ("sec", "tile")
    slots = match_weight.shape[2]

    def flat(s, t):
        return s % n_sec * n_tile + t

    tile_even = [[flat(s, t), flat(s, t + 1)] for s in range(n_sec) for t in range(0, n_tile, 2)]
    tile_odd = [[flat(s, t), flat(s, t + 1)] for s in range(n_sec) for t in range(1, n_tile - 1, 2)]
    sec_even = [[flat(s, t), flat(s + 1, t)] for s in range(0, n_sec, 2) for t in range(n_tile)]
    sec_odd = [[flat(s, t), flat(s + 1, t)] for s in range(1, n_sec - 1, 2) for t in range(n_tile)]
    sec_odd += [[flat(s, t), flat(s, t + 1)] for s in (0, n_sec - 1) for t in range(0, n_tile, 2)]

    def trade_tiles(even, odd):
        swapped = lax.ppermute(odd, axes, [q for a, b in tile_odd for q in ((a, b), (b, a))])
        return lax.all_gather(even, axes, axis_index_groups=tile_even), swapped

    def trade_secs(even, odd):
        even_in = lax.all_gather(even, axes, axis_index_groups=sec_even)
        odd, even_in = lax.optimization_barrier((odd, even_in))
        return even_in, lax.all_gather(odd, axes, axis_index_groups=sec_odd)

    u = displacement[0].reshape(2, 2, 32, LANES).transpose(0, 2, 1, 3).reshape(2, 64, LANES)
    c = stiffness[0].reshape(2, 32, LANES).transpose(1, 0, 2).reshape(64, LANES)
    w, srow, scol, trow, tcol = [a.transpose(1, 0, 2) for a in (match_weight, source_row, source_col, target_row, target_col)]
    off = match_offset[0].transpose(1, 0, 2)
    even, odd, own, ids, u, c = call(
        lambda *r: first_kernel(n_sec, n_tile, *r),
        [((40, LANES), F32), ((40, LANES), F32), ((16, slots), F32), ((16, slots), jnp.int32), ((2, 64, LANES), F32), ((64, LANES), F32)],
        match_count, u, c, w, off, srow, scol, trow, tcol,
        held=True,
    )
    even, odd, mid = call(
        lambda *r: pack_kernel(True, *r), [((120, LANES), F32)] * 2 + [((8, slots), F32)], *trade_secs(even, odd), u, c
    )
    u, share, even, odd = call(
        middle_kernel,
        [((2, 64, LANES), F32), ((64, LANES), F32), ((24, LANES), F32), ((24, LANES), F32)],
        *trade_tiles(even, odd), mid, own, ids, u, c,
    )
    even, odd, mid = call(
        lambda *r: pack_kernel(False, *r), [((80, LANES), F32)] * 2 + [((8, slots), F32)], *trade_secs(even, odd), u, c
    )
    (out,) = call(last_kernel, [((2, 64, LANES), F32)], *trade_tiles(even, odd), mid, own, ids, u, c, share)
    return out.reshape(2, 32, 2, LANES).transpose(0, 2, 1, 3).reshape(1, 2, 2, 32 * LANES)


def solution(mesh):
    placed = (
        P("sec", None, "tile", None),
        P("sec", "tile", None),
        P("sec", "tile", None),
        P("sec", None, "tile", None),
        P("sec", "tile", None),
        P("sec", "tile", None),
        P("sec", "tile", None),
        P("sec", "tile", None),
        P("sec", "tile"),
    )

    def run(*args):
        return body(mesh.shape["sec"], mesh.shape["tile"], *args)

    return jax.shard_map(run, mesh=mesh, in_specs=placed, out_specs=P("sec", None, "tile", None), check_vma=False)
```

```python
import jax
import jax.numpy as jnp
from jax import lax
from jax.experimental import pallas as pl
from jax.experimental.pallas import tpu as pltpu
from jax.sharding import PartitionSpec as P

damping = 0.7
LANES = 128
F32 = jnp.float32
BF16 = jnp.bfloat16
HBM = pl.BlockSpec(memory_space=pltpu.HBM)
VMEM = pl.BlockSpec(memory_space=pltpu.VMEM)


def halves(value):
    high = value.astype(BF16)
    return high, (value - high.astype(F32)).astype(BF16)


def one_hot(index, depth):
    place = lax.broadcasted_iota(jnp.int32, (depth, index.shape[1]), 0)
    return place == index


def lane_one_hot(lane, depth=LANES):
    place = lax.broadcasted_iota(jnp.int32, (depth, LANES), 0).astype(BF16)
    place = jnp.concatenate([place] * (lane.shape[1] // LANES), axis=1)
    return jnp.where(place == lane.astype(BF16), jnp.bfloat16(1), jnp.bfloat16(0))


def wide_rows(rows):
    return jnp.concatenate(rows, axis=1)


def gather(fields, lane_hot, block_mask):
    high, low = halves(jnp.concatenate(fields, axis=0))
    table = jnp.concatenate([high, low], axis=1)
    picked = jnp.dot(table, jnp.concatenate([lane_hot, lane_hot], axis=0), preferred_element_type=F32)
    blocks = block_mask.shape[0]
    return [
        jnp.sum(jnp.where(block_mask, picked[i * blocks : (i + 1) * blocks], 0.0), axis=0, keepdims=True)
        for i in range(len(fields))
    ]


def gather_rows(fields, lane_hot, block_mask):
    high, low = halves(jnp.concatenate([jnp.concatenate([f[:32], f[32:]], axis=1) for f in fields], axis=0))
    picked = jnp.dot(jnp.concatenate([high, low], axis=0), lane_hot, preferred_element_type=F32)
    picked = picked[: high.shape[0]] + picked[high.shape[0] :]
    return [
        jnp.sum(jnp.where(block_mask, picked[32 * i : 32 * i + 32], 0.0), axis=0, keepdims=True)
        for i in range(len(fields))
    ]


def scatter(values, lane_hot, block_hot):
    left = jnp.concatenate([block_hot * v.astype(BF16) for v in values], axis=0)
    return lax.dot_general(left, lane_hot, (((1,), (1,)), ((), ())), preferred_element_type=F32)


def cut(rows):
    pieces = [row[:, LANES * i : LANES * (i + 1)] for row in rows for i in range(row.shape[1] // LANES)]
    return pieces + [jnp.zeros_like(pieces[0])] * ((-len(pieces)) % 8)


def slot_row(block, place):
    return jnp.concatenate([block[4 * place + i : 4 * place + i + 1] for i in range(4)], axis=1)


def side_sum(block):
    count = block.shape[0]
    lane = lax.broadcasted_iota(jnp.int32, block.shape, 1)
    row = lax.broadcasted_iota(jnp.int32, block.shape, 0)
    before = pltpu.roll(block, 1, 1)
    carried = jnp.where(row == 0, 0.0, pltpu.roll(before, 1, 0))
    before = jnp.where(lane == 0, carried, before)
    after = pltpu.roll(block, LANES - 1, 1)
    carried = jnp.where(row == count - 1, 0.0, pltpu.roll(after, count - 1, 0))
    after = jnp.where(lane == LANES - 1, carried, after)
    return before + after


def stencil(above, first, second, below):
    sides = [side_sum(b) for b in (above, first, second, below)]
    upper = first + 0.5 * sides[1]
    lower = second + 0.5 * sides[2]
    return jnp.concatenate(
        [
            above + 0.5 * sides[0] + lower + sides[1],
            upper + below + 0.5 * sides[3] + sides[2],
        ],
        axis=0,
    )


def rows_of(ref, lead=()):
    return [ref[lead + (pl.ds(r, 32, 2), slice(None))] for r in range(2)]


def fill(ref, rows):
    pad = (-len(rows)) % 8
    ref[...] = jnp.concatenate(rows + [jnp.zeros_like(rows[0])] * pad, axis=0)


def send_tiles(odd_tile, left, right, even_ref, odd_ref):
    even_ref[...] = jnp.where(odd_tile, left, right)
    odd_ref[...] = jnp.where(odd_tile, right, left)


def tile_message(halo, slot_rows):
    return jnp.concatenate(halo + cut(slot_rows), axis=0)


def spot():
    return lax.axis_index("sec"), lax.axis_index("tile")


def first_kernel(n_sec, n_tile, *refs):
    far, (even_msg, odd_msg, own, ids, uo, co), held, sems = refs[:9], refs[9:15], refs[15:24], refs[24]
    copies = [pltpu.make_async_copy(f, h, sems.at[i]) for i, (f, h) in enumerate(zip(far, held))]
    for copy in copies:
        copy.start()
    srow, scol, trow, tcol, u, c, w, off, count = held
    for copy in copies[:4]:
        copy.wait()
    sec, tile = spot()
    rows = [(srow[g], scol[g]) for g in range(3)] + [(trow[k], tcol[k]) for k in range(3)]
    blocks = [row * 32 + (col >> 7) for row, col in rows]
    lanes = [col & 127 for row, col in rows]
    lane_hot = lane_one_hot(wide_rows([row * LANES + (col & 127) for row, col in rows]), 2 * LANES)
    block_mask = one_hot(wide_rows([col >> 7 for row, col in rows]), 32)
    for copy in copies[4:]:
        copy.wait()
    field = [jnp.concatenate(rows_of(u, (i,)), axis=0) for i in range(2)]
    stiff = jnp.concatenate(rows_of(c), axis=0)
    for i in range(2):
        uo[i] = field[i]
    co[...] = stiff
    slot = lax.broadcasted_iota(jnp.int32, (1, w.shape[2]), 1)
    got = gather_rows(field, lane_hot, block_mask)
    got = [[v[:, slot.shape[1] * g : slot.shape[1] * (g + 1)] for v in got] for g in range(6)]
    sources = []
    for g in range(3):
        dest = tile + g - 1
        open_group = (sec < n_sec - 1) & (dest >= 0) & (dest < n_tile)
        limit = jnp.where(open_group, count[0:1, g : g + 1], 0)
        weight = jnp.where(slot < limit, w[g], 0.0)
        sources.append([weight * (got[g][i] - off[g, i : i + 1]) for i in range(2)] + [weight])
    targets = got[3:]
    send_secs(sources, targets, even_msg, odd_msg)
    offsets = [off[g, i : i + 1] for g in range(3) for i in range(2)]
    zero = jnp.zeros_like(offsets[0])
    fill(own, [zero] * 5 + [s[2] for s in sources] + offsets)
    fill(ids, blocks + lanes)


def send_secs(sources, targets, even_msg, odd_msg):
    size = even_msg.shape[0]
    source = cut([r for s in sources for r in s])
    target = cut([r for s in targets for r in s])
    zero = jnp.zeros_like(source[0])
    source = jnp.concatenate(source + [zero] * (size - len(source)), axis=0)
    target = jnp.concatenate(target + [zero] * (size - len(target)), axis=0)
    send_tiles((spot()[0] & 1) == 1, target, source, even_msg, odd_msg)


def both_sides(even_in, odd_in, rows):
    parity = spot()[1] & 1
    even = even_in[1 - parity, rows, :]
    odd = odd_in[rows, :]
    return jnp.where(parity == 1, even, odd), jnp.where(parity == 1, odd, even)


def pack_kernel(first, even_in, odd_in, u, c, even_msg, odd_msg, mid):
    n_src = 3 if first else 2
    source, target = arrivals(even_in, odd_in)
    rows = [
        [slot_row(source, n_src * g + i) for i in range(n_src)] + [slot_row(target, 2 * g + i) for i in range(2)]
        for g in range(3)
    ]
    stiff = c[...]
    halo = [stiff * u[0], stiff * u[1]] + ([stiff] if first else [])
    left = tile_message([h[:32] for h in halo], rows[0])
    right = tile_message([h[32:] for h in halo], rows[2])
    send_tiles((spot()[1] & 1) == 1, left, right, even_msg, odd_msg)
    fill(mid, rows[1])


def slot_arrivals(first, even_in, odd_in, mid):
    base = 96 if first else 64
    n_src = 3 if first else 2
    left, right = both_sides(even_in, odd_in, slice(base, even_in.shape[1]))
    sides = [[slot_row(m, i) for i in range(n_src + 2)] for m in (left, right)]
    sides.insert(1, [mid[i : i + 1, :] for i in range(n_src + 2)])
    source = [m[i] for m in sides for i in range(n_src)]
    target = [m[n_src + i] for m in sides for i in range(2)]
    return source, target


def springs(fields, even_in, odd_in):
    up, down = both_sides(even_in, odd_in, slice(0, 32 * len(fields)))
    return [
        stencil(up[32 * i : 32 * i + 32], f[:32], f[32:], down[32 * i : 32 * i + 32])
        for i, f in enumerate(fields)
    ]


def arrivals(even_in, odd_in):
    sec = spot()[0]
    parity = sec & 1
    even, odd = even_in[1 - parity], odd_in[parity]
    source, target = jnp.where(parity == 1, even, odd), jnp.where(parity == 1, odd, even)
    return jnp.where(sec == 0, 0.0, source), target


def offset_rows(own):
    return lambda g, i: own[8 + 2 * g + i : 9 + 2 * g + i, :]


def hots_of(ids):
    lane = wide_rows([ids[6 + g : 7 + g] for g in range(6)])
    block = wide_rows([ids[g : g + 1] for g in range(6)])
    return lane_one_hot(lane), one_hot(block, 64)


def middle_kernel(even_tile, odd_tile, mid, own, ids, u, c, u_out, total_out, even_msg, odd_msg):
    source_in, target_in = slot_arrivals(True, even_tile, odd_tile, mid)
    off = offset_rows(own)
    lane_hot, block_mask = hots_of(ids[...])
    weights = [own[5 + g : 6 + g, :] for g in range(3)]
    values = [
        wide_rows([weights[g] * (target_in[2 * g + i] + off(g, i)) for g in range(3)] + [source_in[3 * k + i] for k in range(3)])
        for i in range(2)
    ]
    values.append(wide_rows(weights + [source_in[3 * k + 2] for k in range(3)]))
    acc = scatter(values, lane_hot, block_mask.astype(BF16))
    stiff = c[...]
    near = springs([stiff * u[0], stiff * u[1], stiff], even_tile, odd_tile)
    share = damping / (stiff * near[2] + acc[128:192])
    total_out[...] = share
    field = [(1.0 - damping) * u[i] + (stiff * near[i] + acc[64 * i : 64 * i + 64]) * share for i in range(2)]
    for i in range(2):
        u_out[i] = field[i]
    got = gather(field, lane_hot, block_mask)
    size = weights[0].shape[1]
    got = [[v[:, size * g : size * (g + 1)] for v in got] for g in range(6)]
    sources = [[weights[g] * (got[g][i] - off(g, i)) for i in range(2)] for g in range(3)]
    send_secs(sources, got[3:], even_msg, odd_msg)


def last_kernel(even_tile, odd_tile, mid, own, ids, u, c, share, out):
    source_in, target_in = slot_arrivals(False, even_tile, odd_tile, mid)
    off = offset_rows(own)
    lane_hot, block_mask = hots_of(ids[...])
    weights = [own[5 + g : 6 + g, :] for g in range(3)]
    values = [
        wide_rows([weights[g] * (target_in[2 * g + i] + off(g, i)) for g in range(3)] + [source_in[2 * k + i] for k in range(3)])
        for i in range(2)
    ]
    acc = scatter(values, lane_hot, block_mask.astype(BF16))
    stiff = c[...]
    near = springs([stiff * u[0], stiff * u[1]], even_tile, odd_tile)
    for i in range(2):
        new = (1.0 - damping) * u[i] + (stiff * near[i] + acc[64 * i : 64 * i + 64]) * share[...]
        for r in range(2):
            out[i, pl.ds(r, 32, 2), :] = new[32 * r : 32 * r + 32]


def call(kernel, shapes, *args, held=False):
    scratch = [pltpu.VMEM(a.shape, a.dtype) for a in args] + [pltpu.SemaphoreType.DMA((len(args),))]
    return pl.pallas_call(
        kernel,
        out_shape=[jax.ShapeDtypeStruct(s, d) for s, d in shapes],
        in_specs=[HBM if held else VMEM] * len(args),
        out_specs=[VMEM] * len(shapes),
        scratch_shapes=scratch if held else [],
        compiler_params=pltpu.CompilerParams(vmem_limit_bytes=32 * 1024 * 1024),
    )(*([pltpu.with_memory_space_constraint(a, pltpu.HBM) for a in args] if held else args))


def body(n_sec, n_tile, displacement, stiffness, match_weight, match_offset, source_row, source_col, target_row, target_col, match_count):
    axes = ("sec", "tile")
    slots = match_weight.shape[2]

    def flat(s, t):
        return s % n_sec * n_tile + t

    tile_even = [[flat(s, t), flat(s, t + 1)] for s in range(n_sec) for t in range(0, n_tile, 2)]
    tile_odd = [[flat(s, t), flat(s, t + 1)] for s in range(n_sec) for t in range(1, n_tile - 1, 2)]
    sec_even = [[flat(s, t), flat(s + 1, t)] for s in range(0, n_sec, 2) for t in range(n_tile)]
    sec_odd = [[flat(s, t), flat(s + 1, t)] for s in range(1, n_sec - 1, 2) for t in range(n_tile)]
    sec_odd += [[flat(s, t), flat(s, t + 1)] for s in (0, n_sec - 1) for t in range(0, n_tile, 2)]

    def trade_tiles(even, odd):
        swapped = lax.ppermute(odd, axes, [q for a, b in tile_odd for q in ((a, b), (b, a))])
        return lax.all_gather(even, axes, axis_index_groups=tile_even), swapped

    def trade_secs(even, odd):
        even_in = lax.all_gather(even, axes, axis_index_groups=sec_even)
        odd, even_in = lax.optimization_barrier((odd, even_in))
        return even_in, lax.all_gather(odd, axes, axis_index_groups=sec_odd)

    u = displacement[0].reshape(2, 2, 32, LANES).transpose(0, 2, 1, 3).reshape(2, 64, LANES)
    c = stiffness[0].reshape(2, 32, LANES).transpose(1, 0, 2).reshape(64, LANES)
    w, srow, scol, trow, tcol = [a.transpose(1, 0, 2) for a in (match_weight, source_row, source_col, target_row, target_col)]
    off = match_offset[0].transpose(1, 0, 2)
    even, odd, own, ids, u, c = call(
        lambda *r: first_kernel(n_sec, n_tile, *r),
        [((40, LANES), F32), ((40, LANES), F32), ((16, slots), F32), ((16, slots), jnp.int32), ((2, 64, LANES), F32), ((64, LANES), F32)],
        srow, scol, trow, tcol, u, c, w, off, match_count,
        held=True,
    )
    even, odd, mid = call(
        lambda *r: pack_kernel(True, *r), [((120, LANES), F32)] * 2 + [((8, slots), F32)], *trade_secs(even, odd), u, c
    )
    u, share, even, odd = call(
        middle_kernel,
        [((2, 64, LANES), F32), ((64, LANES), F32), ((24, LANES), F32), ((24, LANES), F32)],
        *trade_tiles(even, odd), mid, own, ids, u, c,
    )
    even, odd, mid = call(
        lambda *r: pack_kernel(False, *r), [((80, LANES), F32)] * 2 + [((8, slots), F32)], *trade_secs(even, odd), u, c
    )
    (out,) = call(last_kernel, [((2, 64, LANES), F32)], *trade_tiles(even, odd), mid, own, ids, u, c, share)
    return out.reshape(2, 32, 2, LANES).transpose(0, 2, 1, 3).reshape(1, 2, 2, 32 * LANES)


def solution(mesh):
    placed = (
        P("sec", None, "tile", None),
        P("sec", "tile", None),
        P("sec", "tile", None),
        P("sec", None, "tile", None),
        P("sec", "tile", None),
        P("sec", "tile", None),
        P("sec", "tile", None),
        P("sec", "tile", None),
        P("sec", "tile"),
    )

    def run(*args):
        return body(mesh.shape["sec"], mesh.shape["tile"], *args)

    return jax.shard_map(run, mesh=mesh, in_specs=placed, out_specs=P("sec", None, "tile", None), check_vma=False)
```

```python
import jax
import jax.numpy as jnp
from jax import lax
from jax.experimental import pallas as pl
from jax.experimental.pallas import tpu as pltpu
from jax.sharding import PartitionSpec as P

damping = 0.7
LANES = 128
F32 = jnp.float32
BF16 = jnp.bfloat16
HBM = pl.BlockSpec(memory_space=pltpu.HBM)
VMEM = pl.BlockSpec(memory_space=pltpu.VMEM)


def halves(value):
    high = value.astype(BF16)
    return high, (value - high.astype(F32)).astype(BF16)


def one_hot(index, depth):
    place = lax.broadcasted_iota(jnp.int32, (depth, index.shape[1]), 0)
    return place == index


def lane_one_hot(lane):
    place = lax.broadcasted_iota(jnp.int32, (LANES, LANES), 0).astype(BF16)
    place = jnp.concatenate([place] * (lane.shape[1] // LANES), axis=1)
    return jnp.where(place == lane.astype(BF16), jnp.bfloat16(1), jnp.bfloat16(0))


def wide_rows(rows):
    return jnp.concatenate(rows, axis=1)


def gather(fields, lane_hot, block_mask):
    table = jnp.concatenate(fields, axis=0).astype(BF16)
    picked = jnp.dot(table, lane_hot, preferred_element_type=F32)
    blocks = block_mask.shape[0]
    return [
        jnp.sum(jnp.where(block_mask, picked[i * blocks : (i + 1) * blocks], 0.0), axis=0, keepdims=True)
        for i in range(len(fields))
    ]


def scatter(values, lane_hot, block_hot):
    left = jnp.concatenate([block_hot * v.astype(BF16) for v in values], axis=0)
    return lax.dot_general(left, lane_hot, (((1,), (1,)), ((), ())), preferred_element_type=F32)


def cut(rows):
    pieces = [row[:, LANES * i : LANES * (i + 1)] for row in rows for i in range(row.shape[1] // LANES)]
    return pieces + [jnp.zeros_like(pieces[0])] * ((-len(pieces)) % 8)


def slot_row(block, place):
    return jnp.concatenate([block[4 * place + i : 4 * place + i + 1] for i in range(4)], axis=1)


def side_sum(block):
    count = block.shape[0]
    lane = lax.broadcasted_iota(jnp.int32, block.shape, 1)
    row = lax.broadcasted_iota(jnp.int32, block.shape, 0)
    before = pltpu.roll(block, 1, 1)
    carried = jnp.where(row == 0, 0.0, pltpu.roll(before, 1, 0))
    before = jnp.where(lane == 0, carried, before)
    after = pltpu.roll(block, LANES - 1, 1)
    carried = jnp.where(row == count - 1, 0.0, pltpu.roll(after, count - 1, 0))
    after = jnp.where(lane == LANES - 1, carried, after)
    return before + after


def stencil(above, first, second, below):
    sides = [side_sum(b) for b in (above, first, second, below)]
    upper = first + 0.5 * sides[1]
    lower = second + 0.5 * sides[2]
    return jnp.concatenate(
        [
            above + 0.5 * sides[0] + lower + sides[1],
            upper + below + 0.5 * sides[3] + sides[2],
        ],
        axis=0,
    )


def rows_of(ref, lead=()):
    return [ref[lead + (pl.ds(r, 32, 2), slice(None))] for r in range(2)]


def fill(ref, rows):
    pad = (-len(rows)) % 8
    ref[...] = jnp.concatenate(rows + [jnp.zeros_like(rows[0])] * pad, axis=0)


def send_tiles(odd_tile, left, right, even_ref, odd_ref):
    even_ref[...] = jnp.where(odd_tile, left, right)
    odd_ref[...] = jnp.where(odd_tile, right, left)


def tile_message(halo, slot_rows):
    return jnp.concatenate(halo + cut(slot_rows), axis=0)


def spot():
    return lax.axis_index("sec"), lax.axis_index("tile")


def first_kernel(n_sec, n_tile, *refs):
    far, (even_msg, odd_msg, own, ids, uo, co), held, sems = refs[:9], refs[9:15], refs[15:24], refs[24]
    copies = [pltpu.make_async_copy(f, h, sems.at[i]) for i, (f, h) in enumerate(zip(far, held))]
    for copy in copies:
        copy.start()
    for copy in copies:
        copy.wait()
    count, u, c, w, off, srow, scol, trow, tcol = held
    sec, tile = spot()
    field = [jnp.concatenate(rows_of(u, (i,)), axis=0) for i in range(2)]
    stiff = jnp.concatenate(rows_of(c), axis=0)
    for i in range(2):
        uo[i] = field[i]
    co[...] = stiff
    slot = lax.broadcasted_iota(jnp.int32, (1, w.shape[2]), 1)
    rows = [(srow, scol, g) for g in range(3)] + [(trow, tcol, k) for k in range(3)]
    blocks = [row[g] * 32 + (col[g] >> 7) for row, col, g in rows]
    lanes = [col[g] & 127 for row, col, g in rows]
    got = gather(field, lane_one_hot(wide_rows(lanes)), one_hot(wide_rows(blocks), 64))
    got = [[v[:, slot.shape[1] * g : slot.shape[1] * (g + 1)] for v in got] for g in range(6)]
    sources = []
    for g in range(3):
        dest = tile + g - 1
        open_group = (sec < n_sec - 1) & (dest >= 0) & (dest < n_tile)
        limit = jnp.where(open_group, count[0:1, g : g + 1], 0)
        weight = jnp.where(slot < limit, w[g], 0.0)
        sources.append([weight * (got[g][i] - off[g, i : i + 1]) for i in range(2)] + [weight])
    targets = got[3:]
    send_secs(sources, targets, even_msg, odd_msg)
    offsets = [off[g, i : i + 1] for g in range(3) for i in range(2)]
    zero = jnp.zeros_like(offsets[0])
    fill(own, [zero] * 5 + [s[2] for s in sources] + offsets)
    fill(ids, blocks + lanes)


def send_secs(sources, targets, even_msg, odd_msg):
    size = even_msg.shape[0]
    source = cut([r for s in sources for r in s])
    target = cut([r for s in targets for r in s])
    zero = jnp.zeros_like(source[0])
    source = jnp.concatenate(source + [zero] * (size - len(source)), axis=0)
    target = jnp.concatenate(target + [zero] * (size - len(target)), axis=0)
    send_tiles((spot()[0] & 1) == 1, target, source, even_msg, odd_msg)


def both_sides(even_in, odd_in, rows):
    parity = spot()[1] & 1
    even = even_in[1 - parity, rows, :]
    odd = odd_in[rows, :]
    return jnp.where(parity == 1, even, odd), jnp.where(parity == 1, odd, even)


def pack_kernel(first, even_in, odd_in, u, c, even_msg, odd_msg, mid):
    n_src = 3 if first else 2
    source, target = arrivals(even_in, odd_in)
    rows = [
        [slot_row(source, n_src * g + i) for i in range(n_src)] + [slot_row(target, 2 * g + i) for i in range(2)]
        for g in range(3)
    ]
    stiff = c[...]
    halo = [stiff * u[0], stiff * u[1]] + ([stiff] if first else [])
    left = tile_message([h[:32] for h in halo], rows[0])
    right = tile_message([h[32:] for h in halo], rows[2])
    send_tiles((spot()[1] & 1) == 1, left, right, even_msg, odd_msg)
    fill(mid, rows[1])


def slot_arrivals(first, even_in, odd_in, mid):
    base = 96 if first else 64
    n_src = 3 if first else 2
    left, right = both_sides(even_in, odd_in, slice(base, even_in.shape[1]))
    sides = [[slot_row(m, i) for i in range(n_src + 2)] for m in (left, right)]
    sides.insert(1, [mid[i : i + 1, :] for i in range(n_src + 2)])
    source = [m[i] for m in sides for i in range(n_src)]
    target = [m[n_src + i] for m in sides for i in range(2)]
    return source, target


def springs(fields, even_in, odd_in):
    up, down = both_sides(even_in, odd_in, slice(0, 32 * len(fields)))
    return [
        stencil(up[32 * i : 32 * i + 32], f[:32], f[32:], down[32 * i : 32 * i + 32])
        for i, f in enumerate(fields)
    ]


def arrivals(even_in, odd_in):
    sec = spot()[0]
    parity = sec & 1
    even, odd = even_in[1 - parity], odd_in[parity]
    source, target = jnp.where(parity == 1, even, odd), jnp.where(parity == 1, odd, even)
    return jnp.where(sec == 0, 0.0, source), target


def offset_rows(own):
    return lambda g, i: own[8 + 2 * g + i : 9 + 2 * g + i, :]


def hots_of(ids):
    lane = wide_rows([ids[6 + g : 7 + g] for g in range(6)])
    block = wide_rows([ids[g : g + 1] for g in range(6)])
    return lane_one_hot(lane), one_hot(block, 64)


def middle_kernel(even_tile, odd_tile, mid, own, ids, u, c, u_out, total_out, even_msg, odd_msg):
    source_in, target_in = slot_arrivals(True, even_tile, odd_tile, mid)
    off = offset_rows(own)
    lane_hot, block_mask = hots_of(ids[...])
    weights = [own[5 + g : 6 + g, :] for g in range(3)]
    values = [
        wide_rows([weights[g] * (target_in[2 * g + i] + off(g, i)) for g in range(3)] + [source_in[3 * k + i] for k in range(3)])
        for i in range(2)
    ]
    values.append(wide_rows(weights + [source_in[3 * k + 2] for k in range(3)]))
    acc = scatter(values, lane_hot, block_mask.astype(BF16))
    stiff = c[...]
    near = springs([stiff * u[0], stiff * u[1], stiff], even_tile, odd_tile)
    share = damping / (stiff * near[2] + acc[128:192])
    total_out[...] = share
    field = [(1.0 - damping) * u[i] + (stiff * near[i] + acc[64 * i : 64 * i + 64]) * share for i in range(2)]
    for i in range(2):
        u_out[i] = field[i]
    got = gather(field, lane_hot, block_mask)
    size = weights[0].shape[1]
    got = [[v[:, size * g : size * (g + 1)] for v in got] for g in range(6)]
    sources = [[weights[g] * (got[g][i] - off(g, i)) for i in range(2)] for g in range(3)]
    send_secs(sources, got[3:], even_msg, odd_msg)


def last_kernel(even_tile, odd_tile, mid, own, ids, u, c, share, out):
    source_in, target_in = slot_arrivals(False, even_tile, odd_tile, mid)
    off = offset_rows(own)
    lane_hot, block_mask = hots_of(ids[...])
    weights = [own[5 + g : 6 + g, :] for g in range(3)]
    values = [
        wide_rows([weights[g] * (target_in[2 * g + i] + off(g, i)) for g in range(3)] + [source_in[2 * k + i] for k in range(3)])
        for i in range(2)
    ]
    acc = scatter(values, lane_hot, block_mask.astype(BF16))
    stiff = c[...]
    near = springs([stiff * u[0], stiff * u[1]], even_tile, odd_tile)
    for i in range(2):
        new = (1.0 - damping) * u[i] + (stiff * near[i] + acc[64 * i : 64 * i + 64]) * share[...]
        for r in range(2):
            out[i, pl.ds(r, 32, 2), :] = new[32 * r : 32 * r + 32]


def call(kernel, shapes, *args, held=False):
    scratch = [pltpu.VMEM(a.shape, a.dtype) for a in args] + [pltpu.SemaphoreType.DMA((len(args),))]
    return pl.pallas_call(
        kernel,
        out_shape=[jax.ShapeDtypeStruct(s, d) for s, d in shapes],
        in_specs=[HBM if held else VMEM] * len(args),
        out_specs=[VMEM] * len(shapes),
        scratch_shapes=scratch if held else [],
        compiler_params=pltpu.CompilerParams(vmem_limit_bytes=32 * 1024 * 1024),
    )(*([pltpu.with_memory_space_constraint(a, pltpu.HBM) for a in args] if held else args))


def body(n_sec, n_tile, displacement, stiffness, match_weight, match_offset, source_row, source_col, target_row, target_col, match_count):
    axes = ("sec", "tile")
    slots = match_weight.shape[2]

    def flat(s, t):
        return s % n_sec * n_tile + t

    tile_even = [[flat(s, t), flat(s, t + 1)] for s in range(n_sec) for t in range(0, n_tile, 2)]
    tile_odd = [[flat(s, t), flat(s, t + 1)] for s in range(n_sec) for t in range(1, n_tile - 1, 2)]
    sec_even = [[flat(s, t), flat(s + 1, t)] for s in range(0, n_sec, 2) for t in range(n_tile)]
    sec_odd = [[flat(s, t), flat(s + 1, t)] for s in range(1, n_sec - 1, 2) for t in range(n_tile)]
    sec_odd += [[flat(s, t), flat(s, t + 1)] for s in (0, n_sec - 1) for t in range(0, n_tile, 2)]

    def trade_tiles(even, odd):
        swapped = lax.ppermute(odd, axes, [q for a, b in tile_odd for q in ((a, b), (b, a))])
        return lax.all_gather(even, axes, axis_index_groups=tile_even), swapped

    def trade_secs(even, odd):
        even_in = lax.all_gather(even, axes, axis_index_groups=sec_even)
        odd, even_in = lax.optimization_barrier((odd, even_in))
        return even_in, lax.all_gather(odd, axes, axis_index_groups=sec_odd)

    u = displacement[0].reshape(2, 2, 32, LANES).transpose(0, 2, 1, 3).reshape(2, 64, LANES)
    c = stiffness[0].reshape(2, 32, LANES).transpose(1, 0, 2).reshape(64, LANES)
    w, srow, scol, trow, tcol = [a.transpose(1, 0, 2) for a in (match_weight, source_row, source_col, target_row, target_col)]
    off = match_offset[0].transpose(1, 0, 2)
    even, odd, own, ids, u, c = call(
        lambda *r: first_kernel(n_sec, n_tile, *r),
        [((40, LANES), F32), ((40, LANES), F32), ((16, slots), F32), ((16, slots), jnp.int32), ((2, 64, LANES), F32), ((64, LANES), F32)],
        match_count, u, c, w, off, srow, scol, trow, tcol,
        held=True,
    )
    even, odd, mid = call(
        lambda *r: pack_kernel(True, *r), [((120, LANES), F32)] * 2 + [((8, slots), F32)], *trade_secs(even, odd), u, c
    )
    u, share, even, odd = call(
        middle_kernel,
        [((2, 64, LANES), F32), ((64, LANES), F32), ((24, LANES), F32), ((24, LANES), F32)],
        *trade_tiles(even, odd), mid, own, ids, u, c,
    )
    even, odd, mid = call(
        lambda *r: pack_kernel(False, *r), [((80, LANES), F32)] * 2 + [((8, slots), F32)], *trade_secs(even, odd), u, c
    )
    (out,) = call(last_kernel, [((2, 64, LANES), F32)], *trade_tiles(even, odd), mid, own, ids, u, c, share)
    return out.reshape(2, 32, 2, LANES).transpose(0, 2, 1, 3).reshape(1, 2, 2, 32 * LANES)


def solution(mesh):
    placed = (
        P("sec", None, "tile", None),
        P("sec", "tile", None),
        P("sec", "tile", None),
        P("sec", None, "tile", None),
        P("sec", "tile", None),
        P("sec", "tile", None),
        P("sec", "tile", None),
        P("sec", "tile", None),
        P("sec", "tile"),
    )

    def run(*args):
        return body(mesh.shape["sec"], mesh.shape["tile"], *args)

    return jax.shard_map(run, mesh=mesh, in_specs=placed, out_specs=P("sec", None, "tile", None), check_vma=False)
```
